1024 devices in a mesh: head: 2 (over y_lo), inner: 16 (over x, core), outer: 32 (over y_hi, z).
Axes of the slice: x: 8, y: 8 (y_hi: 4, y_lo: 2; y = y_hi * 2 + y_lo), z: 8, core: 2. Of those that a mesh axis runs over, the one named last changes fastest.
Arguments:
- queries: bfloat16 [512, 128, 4096], P(('inner', 'outer'), None, 'head'), may hold values from -2.5 to 2.5
- keys: bfloat16 [512, 128, 512], P(('inner', 'outer'), None, 'head'), may hold values from -2.5 to 2.5
- values: bfloat16 [512, 128, 512], P(('inner', 'outer'), None, 'head'), may hold values from -4 to 4
- grad_out: bfloat16 [512, 128, 4096], P(('inner', 'outer'), None, 'head'), may hold values from -4 to 4
- log_denominator: float32 [512, 128, 32], P(('inner', 'outer'), None, 'head'), may hold values from 6 to 9
- output_row_dot: float32 [512, 128, 32], P(('inner', 'outer'), None, 'head'), may hold values from -32 to 32
- offsets: int32 [512, 2], replicated, may hold values from 0 to 65472, as said below
Outputs:
- grad_query: bfloat16 [512, 128, 4096], P(('inner', 'outer'), 'head')
- grad_key: bfloat16 [512, 128, 512], P(('inner', 'outer'), 'head')
- grad_value: bfloat16 [512, 128, 512], P(('inner', 'outer'), 'head')
The draws below stay inside these ranges and needn't reach their ends.
Inputs may be any that keep to these rules, and one draw needn't show every extreme that they name: `offsets`: row b holds p * 64 and (1023 - p) * 64, where p runs over a permutation of 0 to 511, so that all blocks' positions together are 0 to 65535, each once.
All inputs are finite; a program needn't handle non-finite values.
Results may differ from the reference program's by a relative error of at most 0.0058.
Values may be sent and summed in bfloat16 or wider, within the bound.
A program may use at most 32 MiB of HBM per device.

```python
import math
import jax
import jax.numpy as jnp
from jax import lax

HEAD_WIDTH = 128
QUERY_HEADS = 32
KEY_VALUE_HEADS = 4
BLOCK_TOKENS = 128
INNER_STEPS = 3
OUTER_STEPS = 2
SEQUENCE_BLOCKS = 512
N_INNER = 16
N_OUTER = 32


def draw_offsets(key, part):
    halfway = BLOCK_TOKENS // 2
    order_drawn = jax.random.permutation(jax.random.fold_in(key, 11), SEQUENCE_BLOCKS).astype(jnp.int32)
    early = order_drawn * halfway
    late = (2 * SEQUENCE_BLOCKS - 1 - order_drawn) * halfway
    return jnp.stack([early, late], axis=1).astype(jnp.int32)


def block_scale(key, shape, pieces, least, high):
    level = 1.0
    for dim, blocks in pieces:
        draws = jax.random.uniform(jax.random.fold_in(jax.random.fold_in(key, 6), dim), (blocks,), jnp.float32, least / len(pieces), high / len(pieces))
        level = level * jnp.repeat(jnp.exp(draws), shape[dim] // blocks).reshape((-1,) + (1,) * (len(shape) - 1 - dim))
    return level


def scatter_about(own_key, dims, spread, limit, split=(), held_as=jnp.bfloat16):
    result = spread * jax.random.normal(own_key, dims, jnp.float32)
    if split:
        result = result * block_scale(own_key, dims, split, -0.22, 0.18)
    return jnp.clip(result, -limit, limit).astype(held_as)


def setup_inputs(seed: int = 0) -> dict:
    splits = jax.random.split(jax.random.key(seed), 8)
    queries = scatter_about(splits[0], (SEQUENCE_BLOCKS, BLOCK_TOKENS, QUERY_HEADS * HEAD_WIDTH), 1.0, 2.5, ((0, 512), (2, 2)))
    keys = scatter_about(splits[1], (SEQUENCE_BLOCKS, BLOCK_TOKENS, KEY_VALUE_HEADS * HEAD_WIDTH), 1.0, 2.5, ((0, 512), (2, 2)))
    values = scatter_about(splits[2], (SEQUENCE_BLOCKS, BLOCK_TOKENS, KEY_VALUE_HEADS * HEAD_WIDTH), 1.0, 4.0, ((0, 512), (2, 2)))
    grad_out = scatter_about(splits[3], (SEQUENCE_BLOCKS, BLOCK_TOKENS, QUERY_HEADS * HEAD_WIDTH), 1.0, 4.0, ((0, 512), (2, 2)))
    log_denominator = jnp.clip(6.0 + 3.0 * jax.random.uniform(splits[4], (SEQUENCE_BLOCKS, BLOCK_TOKENS, QUERY_HEADS), jnp.float32) ** block_scale(splits[4], (SEQUENCE_BLOCKS, BLOCK_TOKENS, QUERY_HEADS), ((0, 512), (2, 2)), -0.2, 0.2), 6.0, 9.0)
    output_row_dot = scatter_about(splits[5], (SEQUENCE_BLOCKS, BLOCK_TOKENS, QUERY_HEADS), 8.0, 32.0, ((0, 512), (2, 2)), jnp.float32)
    offsets = draw_offsets(jax.random.fold_in(splits[7], 71), 0)
    return dict(queries=queries, keys=keys, values=values, grad_out=grad_out, log_denominator=log_denominator, output_row_dot=output_row_dot, offsets=offsets)


def block_positions(offsets, tokens_per_block):
    halfway = tokens_per_block // 2
    within = jnp.arange(tokens_per_block, dtype=jnp.int32)
    starts = jnp.where(within[None, :] < halfway, offsets[:, 0:1], offsets[:, 1:2])
    return (starts + (within % halfway)[None, :]).astype(jnp.int32)

def rounded(numbers):
    return lax.optimization_barrier(numbers.astype(jnp.bfloat16)).astype(jnp.float32)

def pair_grads(packed):
    query_heads, grad_heads, norm_heads, dot_heads, query_pos, key_heads, value_heads, key_pos = packed
    scaling = 1.0 / math.sqrt(HEAD_WIDTH)
    query_float = query_heads.astype(jnp.float32)
    grad_float = grad_heads.astype(jnp.float32)
    key_float = key_heads.astype(jnp.float32)
    value_float = value_heads.astype(jnp.float32)
    scores = jnp.einsum('otgjd,ougd->ogjtu', query_float, key_float) * scaling
    visible = key_pos[:, None, None, None, :] <= query_pos[:, None, None, :, None]
    probabilities = jnp.where(visible, jnp.exp(scores - norm_heads[..., None]), 0.0)
    grad_probs = jnp.einsum('otgjd,ougd->ogjtu', grad_float, value_float)
    grad_scores = probabilities * (grad_probs - dot_heads[..., None])
    probs_low = rounded(probabilities)
    scores_low = rounded(grad_scores)
    grad_value = jnp.einsum('ogjtu,otgjd->ougd', probs_low, grad_float)
    grad_key = scaling * jnp.einsum('ogjtu,otgjd->ougd', scores_low, query_float)
    grad_query = scaling * jnp.einsum('ogjtu,ougd->otgjd', scores_low, key_float)
    return (grad_query, grad_key, grad_value)

def reference(queries, keys, values, grad_out, log_denominator, output_row_dot, offsets):
    blocks_all, tokens_per_block, query_cols = queries.shape
    heads_per_group = QUERY_HEADS // KEY_VALUE_HEADS
    query_layout = (N_INNER, N_OUTER, tokens_per_block, KEY_VALUE_HEADS, heads_per_group, HEAD_WIDTH)
    key_layout = (N_INNER, N_OUTER, tokens_per_block, KEY_VALUE_HEADS, HEAD_WIDTH)
    query_all = queries.reshape(query_layout)
    grad_all = grad_out.reshape(query_layout)
    key_all = keys.reshape(key_layout)
    value_all = values.reshape(key_layout)
    log_norm_full = jnp.transpose(log_denominator.reshape(N_INNER, N_OUTER, tokens_per_block, KEY_VALUE_HEADS, heads_per_group), (0, 1, 3, 4, 2))
    row_dot_full = jnp.transpose(output_row_dot.reshape(N_INNER, N_OUTER, tokens_per_block, KEY_VALUE_HEADS, heads_per_group), (0, 1, 3, 4, 2))
    position_all = block_positions(offsets, tokens_per_block).reshape(N_INNER, N_OUTER, tokens_per_block)
    grad_query = jnp.zeros(query_layout, jnp.float32)
    grad_key = jnp.zeros(key_layout, jnp.float32)
    grad_value = jnp.zeros(key_layout, jnp.float32)
    for inner_step in range(INNER_STEPS):
        for outer_step in range(OUTER_STEPS):
            key_here = jnp.roll(key_all, (inner_step, outer_step), axis=(0, 1))
            value_here = jnp.roll(value_all, (inner_step, outer_step), axis=(0, 1))
            pos_here = jnp.roll(position_all, (inner_step, outer_step), axis=(0, 1))
            term_query, term_key, term_value = lax.map(pair_grads, (query_all, grad_all, log_norm_full, row_dot_full, position_all, key_here, value_here, pos_here))
            grad_query = grad_query + term_query
            grad_key = grad_key + jnp.roll(term_key, (-inner_step, -outer_step), axis=(0, 1))
            grad_value = grad_value + jnp.roll(term_value, (-inner_step, -outer_step), axis=(0, 1))
    key_value_columns = KEY_VALUE_HEADS * HEAD_WIDTH
    return (grad_query.astype(jnp.bfloat16).reshape(blocks_all, tokens_per_block, query_cols), grad_key.astype(jnp.bfloat16).reshape(blocks_all, tokens_per_block, key_value_columns), grad_value.astype(jnp.bfloat16).reshape(blocks_all, tokens_per_block, key_value_columns))
```

```python
import functools
import math

import jax
import jax.numpy as jnp
from jax import lax
from jax.experimental import pallas as pl
from jax.experimental.pallas import tpu as pltpu
from jax.sharding import PartitionSpec as P

MESH = pl.DeviceIdType.MESH
F32 = jnp.float32
BF16 = jnp.bfloat16
WIDTH = 128
HALF = 64
GROUPS = 2
SHARED = 8
ROWS = SHARED * HALF
SCALE = 1.0 / math.sqrt(WIDTH)
LOG2E = math.log2(math.e)
HIDDEN = 1.0e5


def product(a, b, dim_a, dim_b):
    return lax.dot_general(
        a, b, (((dim_a,), (dim_b,)), ((), ())), preferred_element_type=F32
    )


def kernel(
    n_inner,
    n_outer,
    q_ref,
    k_ref,
    v_ref,
    do_ref,
    norm_ref,
    dot_ref,
    off_ref,
    oq_ref,
    ok_ref,
    ov_ref,
    q_all,
    do_all,
    q,
    do,
    norm,
    dot,
    dq,
    kv,
    part,
    back,
    got,
    zst,
    zgot,
    hst,
    hgot,
    qst,
    qgot,
    kv_ss,
    kv_rs,
    bk_ss,
    bk_rs,
    z_ss,
    z_rs,
    h_ss,
    h_rs,
    q_ss,
    q_rs,
    in_sem,
):
    i, o, h = lax.axis_index("inner"), lax.axis_index("outer"), lax.axis_index("head")
    other = 1 - h

    def at(di=0, do_=0, head=None):
        return {
            "inner": lax.rem(i + (di + n_inner), n_inner),
            "outer": lax.rem(o + (do_ + n_outer), n_outer),
            "head": h if head is None else head,
        }

    barrier = pltpu.get_barrier_semaphore()
    partners = [at(1), at(-1), at(2), at(-2), at(0, 1), at(0, -1)]
    partners += [at(0, 1, other), at(0, -1, other), at(0, 0, other)]
    for partner in partners:
        pl.semaphore_signal(barrier, inc=1, device_id=partner, device_id_type=MESH)

    loads = []
    for kind, ref in ((0, k_ref), (1, v_ref)):
        for g in range(GROUPS):
            loads.append((ref.at[0, :, pl.ds(g * WIDTH, WIDTH)], kv.at[g, kind, pl.ds(0, WIDTH)]))
    loads += [(q_ref.at[0], q_all), (do_ref.at[0], do_all)]
    loads = [
        pltpu.make_async_copy(source, target, in_sem.at[n])
        for n, (source, target) in enumerate(loads)
    ]
    for load in loads:
        load.start()
    for load in loads[: 2 * GROUPS]:
        load.wait()

    pl.semaphore_wait(barrier, len(partners))

    def slot_copy(source, target, g, device):
        return pltpu.make_async_remote_copy(
            src_ref=kv.at[g, :, pl.ds(source * WIDTH, WIDTH)],
            dst_ref=kv.at[g, :, pl.ds(target * WIDTH, WIDTH)],
            send_sem=kv_ss.at[target - 1, g],
            recv_sem=kv_rs.at[target - 1, g],
            device_id=device,
            device_id_type=MESH,
        )

    def along_outer(g):
        return slot_copy(0, 3, g, at(0, 1))

    def along_inner(row, step, g):
        return slot_copy(3 * row, 3 * row + step, g, at(step))

    def returned(slot, g):
        step = slot % 3
        return pltpu.make_async_remote_copy(
            src_ref=back.at[slot // 3 * 2 + step - 1, g],
            dst_ref=got.at[slot // 3 * 2 + step - 1, g],
            send_sem=bk_ss.at[slot // 3 * 2 + step - 1, g],
            recv_sem=bk_rs.at[slot // 3 * 2 + step - 1, g],
            device_id=at(-step),
            device_id_type=MESH,
        )

    def outer_return(half, g):
        return pltpu.make_async_remote_copy(
            src_ref=zst.at[g, :, pl.ds(half * HALF, HALF)],
            dst_ref=zgot.at[h, g],
            send_sem=z_ss.at[half, g],
            recv_sem=z_rs.at[h, g],
            device_id=at(0, -1, half),
            device_id_type=MESH,
        )

    def outer_arrival(head, g):
        return pltpu.make_async_remote_copy(
            src_ref=zst.at[g, :, pl.ds(0, HALF)],
            dst_ref=zgot.at[head, g],
            send_sem=z_ss.at[0, g],
            recv_sem=z_rs.at[head, g],
            device_id=at(0, -1),
            device_id_type=MESH,
        )

    def head_copy(g):
        return pltpu.make_async_remote_copy(
            src_ref=hst.at[g],
            dst_ref=hgot.at[g],
            send_sem=h_ss.at[g],
            recv_sem=h_rs.at[g],
            device_id=at(0, 0, other),
            device_id_type=MESH,
        )

    def query_copy(g):
        return pltpu.make_async_remote_copy(
            src_ref=qst.at[g],
            dst_ref=qgot.at[g],
            send_sem=q_ss.at[g],
            recv_sem=q_rs.at[g],
            device_id=at(0, 0, other),
            device_id_type=MESH,
        )

    def each_group(body):
        def step(g, carry):
            body(g)
            return carry

        lax.fori_loop(0, GROUPS, step, 0)

    @each_group
    def _(g):
        along_outer(g).start()

    @each_group
    def _(g):
        along_inner(0, 1, g).start()
        along_inner(0, 2, g).start()

    for load in loads[2 * GROUPS :]:
        load.wait()
    for half in range(2):
        rows = slice(half * HALF, (half + 1) * HALF)
        for g in range(GROUPS):
            for j in range(SHARED):
                columns = slice((g * SHARED + j) * WIDTH, (g * SHARED + j + 1) * WIDTH)
                q[half, g, j * HALF : (j + 1) * HALF] = q_all[rows, columns]
                do[half, g, j * HALF : (j + 1) * HALF] = do_all[rows, columns]
    low_lane = lax.broadcasted_iota(jnp.int32, (1, WIDTH), 1) < HALF
    for source, target, factor in ((norm_ref, norm, LOG2E), (dot_ref, dot, 1.0)):
        straight = source[0] * factor
        swapped = pltpu.roll(straight, HALF, 1)
        for g in range(GROUPS):
            for j in range(0, SHARED, 2):
                a, b = g * SHARED + j, g * SHARED + j + 1
                columns = slice(j * HALF, (j + 2) * HALF)
                target[0, g, :, columns] = jnp.where(
                    low_lane, straight[a : a + 1], swapped[b : b + 1]
                )
                target[1, g, :, columns] = jnp.where(
                    low_lane, swapped[a : a + 1], straight[b : b + 1]
                )

    def block_of(slot):
        there = at(-(slot % 3), -(slot // 3))
        return there["inner"] * n_outer + there["outer"]

    def cover(slot, half):
        seen = off_ref[half, block_of(slot)] < off_ref[half, block_of(0)]
        return jnp.where(seen, 0.0, HIDDEN).astype(F32)

    within = lax.broadcasted_iota(jnp.int32, (HALF, ROWS), 0) <= (
        lax.broadcasted_iota(jnp.int32, (HALF, ROWS), 1) % HALF
    )

    def tile(half, g, keys, values, slots, kinds):
        queries, grads = q[half, g], do[half, g]
        bias = norm[half, g]
        scores = product(keys, queries, 1, 1) * (SCALE * LOG2E)
        pieces = []
        for n, (slot, key_half) in enumerate(kinds):
            piece = scores[n * HALF : (n + 1) * HALF]
            if key_half != half:
                piece = jnp.exp2(piece - bias)
            elif slot == 0:
                piece = jnp.where(within, jnp.exp2(piece - bias), 0.0)
            else:
                piece = jnp.exp2(piece - (bias + cover(slot, half)))
            pieces.append(piece)
        probs = jnp.concatenate(pieces, 0)
        grad_probs = product(values, grads, 1, 1)
        grad_scores = (probs * (grad_probs - dot[half, g])).astype(BF16)
        probs = probs.astype(BF16)
        grad_value = product(probs, grads, 1, 0)
        grad_key = product(grad_scores, queries, 1, 0)
        term = product(grad_scores, keys, 0, 0)
        dq[half, g] = term if slots[0] == 0 else dq[half, g] + term
        return grad_key, grad_value

    def compute(slots, g):
        here = pl.ds(slots[0] * WIDTH, len(slots) * WIDTH)
        keys, values = kv[g, 0, here], kv[g, 1, here]
        count = range(len(slots))
        early = lambda x: jnp.concatenate([x[n * WIDTH : n * WIDTH + HALF] for n in count], 0)
        late_side = tile(1, g, keys, values, slots, [(s, kh) for s in slots for kh in (0, 1)])
        early_side = tile(0, g, early(keys), early(values), slots, [(s, 0) for s in slots])
        sums = []
        for n in count:
            both = []
            for a, b in zip(late_side, early_side):
                low = a[n * WIDTH : n * WIDTH + HALF] + b[n * HALF : (n + 1) * HALF]
                both.append((low, a[n * WIDTH + HALF : (n + 1) * WIDTH]))
            sums.append(both)
        return sums

    def put(ref, lead, pair):
        for kind, factor in ((0, SCALE), (1, 1.0)):
            for half in range(2):
                rows = slice(half * HALF, (half + 1) * HALF)
                ref[(*lead, kind, rows)] = (pair[kind][half] * factor).astype(ref.dtype)

    def pair_of_slots(row, g):
        one, two = compute((3 * row + 1, 3 * row + 2), g)
        put(back, (2 * row + 1, g), two)
        returned(3 * row + 2, g).start()
        put(back, (2 * row, g), one)
        returned(3 * row + 1, g).start()

    @each_group
    def _(g):
        put(part, (0, g), compute((0,), g)[0])

    @each_group
    def _(g):
        along_inner(0, 1, g).wait_recv()
        along_inner(0, 2, g).wait_recv()
        pair_of_slots(0, g)
        along_outer(g).wait_recv()
        along_inner(1, 1, g).start()
        along_inner(1, 2, g).start()

    @each_group
    def _(g):
        put(part, (1, g), compute((3,), g)[0])

    def collect(row, g):
        returned(3 * row + 1, g).wait_recv()
        returned(3 * row + 2, g).wait_recv()
        return part[row, g] + got[2 * row, g].astype(F32) + got[2 * row + 1, g].astype(F32)

    @each_group
    def _(g):
        part[0, g] = collect(0, g)
        hst[g] = part[0, g, :, pl.ds(other * HALF, HALF)].astype(BF16)
        head_copy(g).start()

    @each_group
    def _(g):
        along_inner(1, 1, g).wait_recv()
        along_inner(1, 2, g).wait_recv()
        pair_of_slots(1, g)
        first = h * (GROUPS * SHARED * WIDTH) + g * (SHARED * WIDTH)
        for j in range(SHARED):
            rows = slice(j * HALF, (j + 1) * HALF)
            qst[g, :, j * WIDTH : (j + 1) * WIDTH] = (dq[other, g, rows] * SCALE).astype(BF16)
        query_copy(g).start()
        for j in range(SHARED):
            rows = slice(j * HALF, (j + 1) * HALF)
            columns = pl.ds(pl.multiple_of(first + j * WIDTH, WIDTH), WIDTH)
            oq_ref[0, :, columns] = (dq[h, g, rows] * SCALE).astype(BF16)

    @each_group
    def _(g):
        zst[g] = collect(1, g).astype(BF16)
        outer_return(0, g).start()
        outer_return(1, g).start()

    @each_group
    def _(g):
        query_copy(g).wait_recv()
        first = other * (GROUPS * SHARED * WIDTH) + g * (SHARED * WIDTH)
        columns = pl.ds(pl.multiple_of(first, WIDTH), SHARED * WIDTH)
        oq_ref[0, :, columns] = qgot[g]

    @each_group
    def _(g):
        mine = pl.ds(pl.multiple_of(h * (GROUPS * WIDTH) + g * WIDTH, WIDTH), WIDTH)
        theirs = pl.ds(pl.multiple_of(other * (GROUPS * WIDTH) + g * WIDTH, WIDTH), WIDTH)
        head_copy(g).wait_recv()
        outer_arrival(0, g).wait_recv()
        outer_arrival(1, g).wait_recv()
        for kind, ref in ((0, ok_ref), (1, ov_ref)):
            own = part[0, g, kind, pl.ds(h * HALF, HALF)] + zgot[h, g, kind].astype(F32)
            ref[0, :, mine] = own.astype(BF16)
            far = hgot[g, kind].astype(F32) + zgot[other, g, kind].astype(F32)
            ref[0, :, theirs] = far.astype(BF16)

    @each_group
    def _(g):
        along_outer(g).wait_send()
        for row in range(2):
            for step in (1, 2):
                along_inner(row, step, g).wait_send()
                returned(3 * row + step, g).wait_send()
        head_copy(g).wait_send()
        query_copy(g).wait_send()
        outer_return(0, g).wait_send()
        outer_return(1, g).wait_send()


def solution(mesh):
    n_inner, n_outer = mesh.shape["inner"], mesh.shape["outer"]
    vmem = pl.BlockSpec(memory_space=pltpu.VMEM)
    hbm = pl.BlockSpec(memory_space=pltpu.HBM)
    square = (2, WIDTH, WIDTH)
    part_half = (2, HALF, WIDTH)
    dma = pltpu.SemaphoreType.DMA

    def shards(queries, keys, values, grad_out, log_denominator, row_dot, offsets):
        columns = GROUPS * SHARED * WIDTH
        return pl.pallas_call(
            functools.partial(kernel, n_inner, n_outer),
            out_shape=[
                jax.ShapeDtypeStruct((1, HALF, 2 * columns), BF16),
                jax.ShapeDtypeStruct((1, HALF, 2 * GROUPS * WIDTH), BF16),
                jax.ShapeDtypeStruct((1, HALF, 2 * GROUPS * WIDTH), BF16),
            ],
            in_specs=[hbm] * 4 + [vmem] * 2 + [pl.BlockSpec(memory_space=pltpu.SMEM)],
            out_specs=[vmem] * 3,
            scratch_shapes=[
                pltpu.VMEM((WIDTH, columns), BF16),
                pltpu.VMEM((WIDTH, columns), BF16),
                pltpu.VMEM((2, GROUPS, ROWS, WIDTH), BF16),
                pltpu.VMEM((2, GROUPS, ROWS, WIDTH), BF16),
                pltpu.VMEM((2, GROUPS, 1, ROWS), F32),
                pltpu.VMEM((2, GROUPS, 1, ROWS), F32),
                pltpu.VMEM((2, GROUPS, ROWS, WIDTH), F32),
                pltpu.VMEM((GROUPS, 2, 6 * WIDTH, WIDTH), BF16),
                pltpu.VMEM((2, GROUPS, *square), F32),
                pltpu.VMEM((4, GROUPS, *square), BF16),
                pltpu.VMEM((4, GROUPS, *square), BF16),
                pltpu.VMEM((GROUPS, *square), BF16),
                pltpu.VMEM((2, GROUPS, *part_half), BF16),
                pltpu.VMEM((GROUPS, *part_half), BF16),
                pltpu.VMEM((GROUPS, *part_half), BF16),
                pltpu.VMEM((GROUPS, HALF, SHARED * WIDTH), BF16),
                pltpu.VMEM((GROUPS, HALF, SHARED * WIDTH), BF16),
                dma((5, GROUPS)),
                dma((5, GROUPS)),
                dma((4, GROUPS)),
                dma((4, GROUPS)),
                dma((2, GROUPS)),
                dma((2, GROUPS)),
                dma((GROUPS,)),
                dma((GROUPS,)),
                dma((GROUPS,)),
                dma((GROUPS,)),
                dma((2 * GROUPS + 2,)),
            ],
            compiler_params=pltpu.CompilerParams(
                collective_id=0, has_side_effects=True, vmem_limit_bytes=60 << 20
            ),
        )(
            queries,
            keys,
            values,
            grad_out,
            jnp.swapaxes(log_denominator, 1, 2),
            jnp.swapaxes(row_dot, 1, 2),
            offsets.T,
        )

    spec_in = P(("inner", "outer"), None, "head")
    spec_out = P(("inner", "outer"), "head", None)
    return jax.shard_map(
        shards,
        mesh=mesh,
        in_specs=(spec_in,) * 6 + (P(),),
        out_specs=(spec_out,) * 3,
        check_vma=False,
    )
```

```python
import functools
import math

import jax
import jax.numpy as jnp
from jax import lax
from jax.experimental import pallas as pl
from jax.experimental.pallas import tpu as pltpu
from jax.sharding import PartitionSpec as P

MESH = pl.DeviceIdType.MESH
F32 = jnp.float32
BF16 = jnp.bfloat16
WIDTH = 128
HALF = 64
GROUPS = 2
SHARED = 8
ROWS = SHARED * HALF
SCALE = 1.0 / math.sqrt(WIDTH)
LOG2E = math.log2(math.e)
DEPTH = 8
HIDDEN = 1.0e5


def product(a, b, dim_a, dim_b):
    return lax.dot_general(
        a, b, (((dim_a,), (dim_b,)), ((), ())), preferred_element_type=F32
    )


def kernel(
    n_inner,
    n_outer,
    q_ref,
    k_ref,
    v_ref,
    do_ref,
    norm_ref,
    dot_ref,
    off_ref,
    oq_ref,
    ok_ref,
    ov_ref,
    q_all,
    do_all,
    q,
    do,
    norm,
    dot,
    dq,
    kv,
    part,
    back,
    got,
    zst,
    relay,
    zgot,
    hst,
    hgot,
    qst,
    qgot,
    kv_ss,
    kv_rs,
    bk_ss,
    bk_rs,
    z_ss,
    z_rs,
    h_ss,
    h_rs,
    q_ss,
    q_rs,
    r_ss,
    r_rs,
    f_ss,
    in_sem,
):
    i, o, h = lax.axis_index("inner"), lax.axis_index("outer"), lax.axis_index("head")
    other = 1 - h

    def at(di=0, do_=0, head=None):
        return {
            "inner": lax.rem(i + (di + n_inner), n_inner),
            "outer": lax.rem(o + (do_ + n_outer), n_outer),
            "head": h if head is None else head,
        }

    loads = []
    for kind, ref in ((0, k_ref), (1, v_ref)):
        for g in range(GROUPS):
            loads.append((ref.at[0, :, pl.ds(g * WIDTH, WIDTH)], kv.at[g, kind, pl.ds(0, WIDTH)]))
    loads += [(q_ref.at[0], q_all), (do_ref.at[0], do_all)]
    loads = [
        pltpu.make_async_copy(source, target, in_sem.at[n])
        for n, (source, target) in enumerate(loads)
    ]
    for load in loads:
        load.start()

    barrier = pltpu.get_barrier_semaphore()
    partners = [at(1), at(-1), at(2), at(-2), at(0, 1), at(0, -1)]
    partners += [at(0, 1, other), at(0, -1, other), at(0, 0, other)]
    place = lax.rem(o, DEPTH)
    first_of_row, last_of_row = place == 0, place == DEPTH - 1
    relays_first = [at(0, DEPTH - 1)]
    relays_last = [at(0, 1 - DEPTH)] + [at(0, d, side) for d in (-DEPTH, DEPTH) for side in (0, 1)]

    def greet(devices):
        for device in devices:
            pl.semaphore_signal(barrier, inc=1, device_id=device, device_id_type=MESH)

    greet(partners)

    @pl.when(first_of_row)
    def _():
        greet(relays_first)

    @pl.when(last_of_row)
    def _():
        greet(relays_last)

    for load in loads[: 2 * GROUPS]:
        load.wait()

    more = jnp.where(first_of_row, len(relays_first), 0) + jnp.where(last_of_row, len(relays_last), 0)
    pl.semaphore_wait(barrier, len(partners) + more)

    def slot_copy(source, target, g, device):
        return pltpu.make_async_remote_copy(
            src_ref=kv.at[g, :, pl.ds(source * WIDTH, WIDTH)],
            dst_ref=kv.at[g, :, pl.ds(target * WIDTH, WIDTH)],
            send_sem=kv_ss.at[target - 1, g],
            recv_sem=kv_rs.at[target - 1, g],
            device_id=device,
            device_id_type=MESH,
        )

    def along_outer(g):
        return slot_copy(0, 3, g, at(0, 1))

    def along_inner(row, step, g):
        return slot_copy(3 * row, 3 * row + step, g, at(step))

    def returned(slot, g):
        step = slot % 3
        return pltpu.make_async_remote_copy(
            src_ref=back.at[slot // 3 * 2 + step - 1, g],
            dst_ref=got.at[slot // 3 * 2 + step - 1, g],
            send_sem=bk_ss.at[slot // 3 * 2 + step - 1, g],
            recv_sem=bk_rs.at[slot // 3 * 2 + step - 1, g],
            device_id=at(-step),
            device_id_type=MESH,
        )

    def outer_return(half, g):
        return pltpu.make_async_remote_copy(
            src_ref=zst.at[g, :, pl.ds(half * HALF, HALF)],
            dst_ref=zgot.at[h, g],
            send_sem=z_ss.at[half, g],
            recv_sem=z_rs.at[h, g],
            device_id=at(0, -1, half),
            device_id_type=MESH,
        )

    def outer_arrival(head, g):
        return pltpu.make_async_remote_copy(
            src_ref=zst.at[g, :, pl.ds(0, HALF)],
            dst_ref=zgot.at[head, g],
            send_sem=z_ss.at[0, g],
            recv_sem=z_rs.at[head, g],
            device_id=at(0, -1),
            device_id_type=MESH,
        )

    def relay_copy(g):
        return pltpu.make_async_remote_copy(
            src_ref=zst.at[g],
            dst_ref=relay.at[g],
            send_sem=r_ss.at[g],
            recv_sem=r_rs.at[g],
            device_id=at(0, DEPTH - 1),
            device_id_type=MESH,
        )

    def relay_onward(half, g):
        return pltpu.make_async_remote_copy(
            src_ref=relay.at[g, :, pl.ds(half * HALF, HALF)],
            dst_ref=zgot.at[h, g],
            send_sem=f_ss.at[half, g],
            recv_sem=z_rs.at[h, g],
            device_id=at(0, -DEPTH, half),
            device_id_type=MESH,
        )

    def head_copy(g):
        return pltpu.make_async_remote_copy(
            src_ref=hst.at[g],
            dst_ref=hgot.at[g],
            send_sem=h_ss.at[g],
            recv_sem=h_rs.at[g],
            device_id=at(0, 0, other),
            device_id_type=MESH,
        )

    def query_copy(g):
        return pltpu.make_async_remote_copy(
            src_ref=qst.at[g],
            dst_ref=qgot.at[g],
            send_sem=q_ss.at[g],
            recv_sem=q_rs.at[g],
            device_id=at(0, 0, other),
            device_id_type=MESH,
        )

    def each_group(body):
        def step(g, carry):
            body(g)
            return carry

        lax.fori_loop(0, GROUPS, step, 0)

    along_outer(0).start()

    @each_group
    def _(g):
        along_inner(0, 2, g).start()
        along_inner(0, 1, g).start()

    for load in loads[2 * GROUPS :]:
        load.wait()
    for half in range(2):
        rows = slice(half * HALF, (half + 1) * HALF)
        for g in range(GROUPS):
            for j in range(SHARED):
                columns = slice((g * SHARED + j) * WIDTH, (g * SHARED + j + 1) * WIDTH)
                q[half, g, j * HALF : (j + 1) * HALF] = q_all[rows, columns]
                do[half, g, j * HALF : (j + 1) * HALF] = do_all[rows, columns]
    low_lane = lax.broadcasted_iota(jnp.int32, (1, WIDTH), 1) < HALF
    for source, target, factor in ((norm_ref, norm, LOG2E), (dot_ref, dot, 1.0)):
        straight = source[0] * factor
        swapped = pltpu.roll(straight, HALF, 1)
        for g in range(GROUPS):
            for j in range(0, SHARED, 2):
                a, b = g * SHARED + j, g * SHARED + j + 1
                columns = slice(j * HALF, (j + 2) * HALF)
                target[0, g, :, columns] = jnp.where(
                    low_lane, straight[a : a + 1], swapped[b : b + 1]
                )
                target[1, g, :, columns] = jnp.where(
                    low_lane, swapped[a : a + 1], straight[b : b + 1]
                )

    def block_of(slot):
        there = at(-(slot % 3), -(slot // 3))
        return there["inner"] * n_outer + there["outer"]

    def cover(slot, half):
        seen = off_ref[half, block_of(slot)] < off_ref[half, block_of(0)]
        return jnp.where(seen, 0.0, HIDDEN).astype(F32)

    within = lax.broadcasted_iota(jnp.int32, (HALF, ROWS), 0) <= (
        lax.broadcasted_iota(jnp.int32, (HALF, ROWS), 1) % HALF
    )

    def tile(half, g, keys, values, slots, kinds):
        queries, grads = q[half, g], do[half, g]
        bias = norm[half, g]
        scores = product(keys, queries, 1, 1) * (SCALE * LOG2E)
        pieces = []
        for n, (slot, key_half) in enumerate(kinds):
            piece = scores[n * HALF : (n + 1) * HALF]
            if key_half != half:
                piece = jnp.exp2(piece - bias)
            elif slot == 0:
                piece = jnp.where(within, jnp.exp2(piece - bias), 0.0)
            else:
                piece = jnp.exp2(piece - (bias + cover(slot, half)))
            pieces.append(piece)
        probs = jnp.concatenate(pieces, 0)
        grad_probs = product(values, grads, 1, 1)
        grad_scores = (probs * (grad_probs - dot[half, g])).astype(BF16)
        probs = probs.astype(BF16)
        grad_value = product(probs, grads, 1, 0)
        grad_key = product(grad_scores, queries, 1, 0)
        term = product(grad_scores, keys, 0, 0)
        dq[half, g] = term if slots[0] == 0 else dq[half, g] + term
        return grad_key, grad_value

    def compute(slots, g):
        here = pl.ds(slots[0] * WIDTH, len(slots) * WIDTH)
        keys, values = kv[g, 0, here], kv[g, 1, here]
        count = range(len(slots))
        early = lambda x: jnp.concatenate([x[n * WIDTH : n * WIDTH + HALF] for n in count], 0)
        late_side = tile(1, g, keys, values, slots, [(s, kh) for s in slots for kh in (0, 1)])
        early_side = tile(0, g, early(keys), early(values), slots, [(s, 0) for s in slots])
        sums = []
        for n in count:
            both = []
            for a, b in zip(late_side, early_side):
                low = a[n * WIDTH : n * WIDTH + HALF] + b[n * HALF : (n + 1) * HALF]
                both.append((low, a[n * WIDTH + HALF : (n + 1) * WIDTH]))
            sums.append(both)
        return sums

    def put(ref, lead, pair):
        for kind, factor in ((0, SCALE), (1, 1.0)):
            for half in range(2):
                rows = slice(half * HALF, (half + 1) * HALF)
                ref[(*lead, kind, rows)] = (pair[kind][half] * factor).astype(ref.dtype)

    def pair_of_slots(row, g):
        one, two = compute((3 * row + 1, 3 * row + 2), g)
        put(back, (2 * row + 1, g), two)
        returned(3 * row + 2, g).start()
        put(back, (2 * row, g), one)
        returned(3 * row + 1, g).start()

    along_outer(0).wait_send()
    along_outer(1).start()

    @each_group
    def _(g):
        put(part, (0, g), compute((0,), g)[0])

    @each_group
    def _(g):
        along_inner(0, 1, g).wait_recv()
        along_inner(0, 2, g).wait_recv()
        pair_of_slots(0, g)

    @each_group
    def _(g):
        along_outer(g).wait_recv()
        along_inner(1, 2, g).start()
        along_inner(1, 1, g).start()

    @each_group
    def _(g):
        put(part, (1, g), compute((3,), g)[0])

    def collect(row, g):
        returned(3 * row + 1, g).wait_recv()
        returned(3 * row + 2, g).wait_recv()
        return part[row, g] + got[2 * row, g].astype(F32) + got[2 * row + 1, g].astype(F32)

    @each_group
    def _(g):
        part[0, g] = collect(0, g)
        hst[g] = part[0, g, :, pl.ds(other * HALF, HALF)].astype(BF16)
        head_copy(g).start()

    @each_group
    def _(g):
        along_inner(1, 1, g).wait_recv()
        along_inner(1, 2, g).wait_recv()
        pair_of_slots(1, g)
        first = h * (GROUPS * SHARED * WIDTH) + g * (SHARED * WIDTH)
        for j in range(SHARED):
            rows = slice(j * HALF, (j + 1) * HALF)
            qst[g, :, j * WIDTH : (j + 1) * WIDTH] = (dq[other, g, rows] * SCALE).astype(BF16)
        query_copy(g).start()
        for j in range(SHARED):
            rows = slice(j * HALF, (j + 1) * HALF)
            columns = pl.ds(pl.multiple_of(first + j * WIDTH, WIDTH), WIDTH)
            oq_ref[0, :, columns] = (dq[h, g, rows] * SCALE).astype(BF16)

    @each_group
    def _(g):
        zst[g] = collect(1, g).astype(BF16)

        @pl.when(first_of_row)
        def _():
            relay_copy(g).start()

        @pl.when(jnp.logical_not(first_of_row))
        def _():
            outer_return(0, g).start()
            outer_return(1, g).start()

    @each_group
    def _(g):
        query_copy(g).wait_recv()
        first = other * (GROUPS * SHARED * WIDTH) + g * (SHARED * WIDTH)
        columns = pl.ds(pl.multiple_of(first, WIDTH), SHARED * WIDTH)
        oq_ref[0, :, columns] = qgot[g]

    @pl.when(last_of_row)
    def _():
        @each_group
        def _(g):
            relay_copy(g).wait_recv()
            relay_onward(0, g).start()
            relay_onward(1, g).start()

    @each_group
    def _(g):
        mine = pl.ds(pl.multiple_of(h * (GROUPS * WIDTH) + g * WIDTH, WIDTH), WIDTH)
        theirs = pl.ds(pl.multiple_of(other * (GROUPS * WIDTH) + g * WIDTH, WIDTH), WIDTH)
        head_copy(g).wait_recv()
        outer_arrival(0, g).wait_recv()
        outer_arrival(1, g).wait_recv()
        for kind, ref in ((0, ok_ref), (1, ov_ref)):
            own = part[0, g, kind, pl.ds(h * HALF, HALF)] + zgot[h, g, kind].astype(F32)
            ref[0, :, mine] = own.astype(BF16)
            far = hgot[g, kind].astype(F32) + zgot[other, g, kind].astype(F32)
            ref[0, :, theirs] = far.astype(BF16)

    along_outer(1).wait_send()

    @each_group
    def _(g):
        for row in range(2):
            for step in (1, 2):
                along_inner(row, step, g).wait_send()
                returned(3 * row + step, g).wait_send()
        head_copy(g).wait_send()
        query_copy(g).wait_send()

        @pl.when(first_of_row)
        def _():
            relay_copy(g).wait_send()

        @pl.when(jnp.logical_not(first_of_row))
        def _():
            outer_return(0, g).wait_send()
            outer_return(1, g).wait_send()

        @pl.when(last_of_row)
        def _():
            relay_onward(0, g).wait_send()
            relay_onward(1, g).wait_send()


def place_kernel(*refs):
    count = (len(refs) - 1) // 2
    copies = [
        pltpu.make_async_copy(refs[n], refs[count + n], refs[-1].at[n]) for n in range(count)
    ]
    for copy in copies:
        copy.start()
    for copy in copies:
        copy.wait()


def solution(mesh):
    n_inner, n_outer = mesh.shape["inner"], mesh.shape["outer"]
    vmem = pl.BlockSpec(memory_space=pltpu.VMEM)
    hbm = pl.BlockSpec(memory_space=pltpu.HBM)
    square = (2, WIDTH, WIDTH)
    part_half = (2, HALF, WIDTH)
    dma = pltpu.SemaphoreType.DMA

    def shards(queries, keys, values, grad_out, log_denominator, row_dot, offsets):
        columns = GROUPS * SHARED * WIDTH
        shapes = [
            jax.ShapeDtypeStruct((1, HALF, 2 * columns), BF16),
            jax.ShapeDtypeStruct((1, HALF, 2 * GROUPS * WIDTH), BF16),
            jax.ShapeDtypeStruct((1, HALF, 2 * GROUPS * WIDTH), BF16),
        ]
        sums = pl.pallas_call(
            functools.partial(kernel, n_inner, n_outer),
            out_shape=[pltpu.VMEM(shape.shape, shape.dtype) for shape in shapes],
            in_specs=[hbm] * 4 + [vmem] * 2 + [pl.BlockSpec(memory_space=pltpu.SMEM)],
            out_specs=[vmem] * 3,
            scratch_shapes=[
                pltpu.VMEM((WIDTH, columns), BF16),
                pltpu.VMEM((WIDTH, columns), BF16),
                pltpu.VMEM((2, GROUPS, ROWS, WIDTH), BF16),
                pltpu.VMEM((2, GROUPS, ROWS, WIDTH), BF16),
                pltpu.VMEM((2, GROUPS, 1, ROWS), F32),
                pltpu.VMEM((2, GROUPS, 1, ROWS), F32),
                pltpu.VMEM((2, GROUPS, ROWS, WIDTH), F32),
                pltpu.VMEM((GROUPS, 2, 6 * WIDTH, WIDTH), BF16),
                pltpu.VMEM((2, GROUPS, *square), F32),
                pltpu.VMEM((4, GROUPS, *square), BF16),
                pltpu.VMEM((4, GROUPS, *square), BF16),
                pltpu.VMEM((GROUPS, *square), BF16),
                pltpu.VMEM((GROUPS, *square), BF16),
                pltpu.VMEM((2, GROUPS, *part_half), BF16),
                pltpu.VMEM((GROUPS, *part_half), BF16),
                pltpu.VMEM((GROUPS, *part_half), BF16),
                pltpu.VMEM((GROUPS, HALF, SHARED * WIDTH), BF16),
                pltpu.VMEM((GROUPS, HALF, SHARED * WIDTH), BF16),
                dma((5, GROUPS)),
                dma((5, GROUPS)),
                dma((4, GROUPS)),
                dma((4, GROUPS)),
                dma((2, GROUPS)),
                dma((2, GROUPS)),
                dma((GROUPS,)),
                dma((GROUPS,)),
                dma((GROUPS,)),
                dma((GROUPS,)),
                dma((GROUPS,)),
                dma((GROUPS,)),
                dma((2, GROUPS)),
                dma((2 * GROUPS + 2,)),
            ],
            compiler_params=pltpu.CompilerParams(
                collective_id=0, has_side_effects=True, vmem_limit_bytes=56 << 20
            ),
        )(
            queries,
            keys,
            values,
            grad_out,
            jnp.swapaxes(log_denominator, 1, 2),
            jnp.swapaxes(row_dot, 1, 2),
            offsets.T,
        )
        return pl.pallas_call(
            place_kernel,
            out_shape=shapes,
            in_specs=[vmem] * 3,
            out_specs=[pl.BlockSpec(memory_space=pl.ANY)] * 3,
            scratch_shapes=[dma((3,))],
            compiler_params=pltpu.CompilerParams(vmem_limit_bytes=4 << 20),
        )(*sums)

    spec_in = P(("inner", "outer"), None, "head")
    spec_out = P(("inner", "outer"), "head", None)
    return jax.shard_map(
        shards,
        mesh=mesh,
        in_specs=(spec_in,) * 6 + (P(),),
        out_specs=(spec_out,) * 3,
        check_vma=False,
    )
```

```python
import functools
import math

import jax
import jax.numpy as jnp
from jax import lax
from jax.experimental import pallas as pl
from jax.experimental.pallas import tpu as pltpu
from jax.sharding import PartitionSpec as P

MESH = pl.DeviceIdType.MESH
F32 = jnp.float32
BF16 = jnp.bfloat16
WIDTH = 128
HALF = 64
GROUPS = 2
SHARED = 8
ROWS = SHARED * HALF
SCALE = 1.0 / math.sqrt(WIDTH)
LOG2E = math.log2(math.e)
DEPTH = 8
HIDDEN = 1.0e5


def product(a, b, dim_a, dim_b):
    return lax.dot_general(
        a, b, (((dim_a,), (dim_b,)), ((), ())), preferred_element_type=F32
    )


def kernel(
    n_inner,
    n_outer,
    q_ref,
    k_ref,
    v_ref,
    do_ref,
    norm_ref,
    dot_ref,
    off_ref,
    oq_ref,
    ok_ref,
    ov_ref,
    q_all,
    do_all,
    q,
    do,
    norm,
    dot,
    dq,
    kv,
    part,
    back,
    got,
    zst,
    relay,
    zgot,
    hst,
    hgot,
    qst,
    qgot,
    kv_ss,
    kv_rs,
    bk_ss,
    bk_rs,
    z_ss,
    z_rs,
    h_ss,
    h_rs,
    q_ss,
    q_rs,
    r_ss,
    r_rs,
    f_ss,
    ready,
    in_sem,
):
    i, o, h = lax.axis_index("inner"), lax.axis_index("outer"), lax.axis_index("head")
    other = 1 - h

    def at(di=0, do_=0, head=None):
        return {
            "inner": lax.rem(i + (di + n_inner), n_inner),
            "outer": lax.rem(o + (do_ + n_outer), n_outer),
            "head": h if head is None else head,
        }

    loads = []
    for kind, ref in ((0, k_ref), (1, v_ref)):
        for g in range(GROUPS):
            loads.append((ref.at[0, :, pl.ds(g * WIDTH, WIDTH)], kv.at[g, kind, pl.ds(0, WIDTH)]))
    loads += [(q_ref.at[0], q_all), (do_ref.at[0], do_all)]
    loads = [
        pltpu.make_async_copy(source, target, in_sem.at[n])
        for n, (source, target) in enumerate(loads)
    ]
    for load in loads:
        load.start()

    barrier = pltpu.get_barrier_semaphore()
    place = lax.rem(o, DEPTH)
    first_of_row, last_of_row = place == 0, place == DEPTH - 1
    not_first, not_last = jnp.logical_not(first_of_row), jnp.logical_not(last_of_row)

    def greet(devices):
        for device in devices:
            pl.semaphore_signal(barrier, inc=1, device_id=device, device_id_type=MESH)

    greet([at(0, -1), at(0, 0, other), at(1), at(-1), at(2), at(-2)])

    @pl.when(not_last)
    def _():
        greet([at(0, 1), at(0, 1, other)])

    @pl.when(first_of_row)
    def _():
        greet([at(0, DEPTH - 1)])

    @pl.when(last_of_row)
    def _():
        greet([at(0, DEPTH, 0), at(0, DEPTH, 1)])

    for load in loads[: 2 * GROUPS]:
        load.wait()

    greeted = 6 + jnp.where(not_first, 2, 0) + jnp.where(last_of_row, 3, 0)
    pl.semaphore_wait(barrier, greeted)

    def slot_copy(source, target, g, device):
        return pltpu.make_async_remote_copy(
            src_ref=kv.at[g, :, pl.ds(source * WIDTH, WIDTH)],
            dst_ref=kv.at[g, :, pl.ds(target * WIDTH, WIDTH)],
            send_sem=kv_ss.at[target - 1, g],
            recv_sem=kv_rs.at[target - 1, g],
            device_id=device,
            device_id_type=MESH,
        )

    def along_outer(g):
        return slot_copy(0, 3, g, at(0, 1))

    def along_inner(row, step, g):
        return slot_copy(3 * row, 3 * row + step, g, at(step))

    def returned(slot, g):
        step = slot % 3
        return pltpu.make_async_remote_copy(
            src_ref=back.at[slot // 3 * 2 + step - 1, g],
            dst_ref=got.at[slot // 3 * 2 + step - 1, g],
            send_sem=bk_ss.at[slot // 3 * 2 + step - 1, g],
            recv_sem=bk_rs.at[slot // 3 * 2 + step - 1, g],
            device_id=at(-step),
            device_id_type=MESH,
        )

    def outer_return(half, g):
        return pltpu.make_async_remote_copy(
            src_ref=zst.at[g, :, pl.ds(half * HALF, HALF)],
            dst_ref=zgot.at[h, g],
            send_sem=z_ss.at[half, g],
            recv_sem=z_rs.at[h, g],
            device_id=at(0, -1, half),
            device_id_type=MESH,
        )

    def outer_arrival(head, g):
        return pltpu.make_async_remote_copy(
            src_ref=zst.at[g, :, pl.ds(0, HALF)],
            dst_ref=zgot.at[head, g],
            send_sem=z_ss.at[0, g],
            recv_sem=z_rs.at[head, g],
            device_id=at(0, -1),
            device_id_type=MESH,
        )

    def relay_copy(g):
        return pltpu.make_async_remote_copy(
            src_ref=zst.at[g],
            dst_ref=relay.at[g],
            send_sem=r_ss.at[g],
            recv_sem=r_rs.at[g],
            device_id=at(0, DEPTH - 1),
            device_id_type=MESH,
        )

    def relay_onward(half, g):
        return pltpu.make_async_remote_copy(
            src_ref=relay.at[g, :, pl.ds(half * HALF, HALF)],
            dst_ref=zgot.at[h, g],
            send_sem=f_ss.at[half, g],
            recv_sem=z_rs.at[h, g],
            device_id=at(0, -DEPTH, half),
            device_id_type=MESH,
        )

    def head_copy(g):
        return pltpu.make_async_remote_copy(
            src_ref=hst.at[g],
            dst_ref=hgot.at[g],
            send_sem=h_ss.at[g],
            recv_sem=h_rs.at[g],
            device_id=at(0, 0, other),
            device_id_type=MESH,
        )

    def query_copy(g):
        return pltpu.make_async_remote_copy(
            src_ref=qst.at[g],
            dst_ref=qgot.at[g],
            send_sem=q_ss.at[g],
            recv_sem=q_rs.at[g],
            device_id=at(0, 0, other),
            device_id_type=MESH,
        )

    def each_group(body):
        def step(g, carry):
            body(g)
            return carry

        lax.fori_loop(0, GROUPS, step, 0)

    along_outer(0).start()

    @pl.when(last_of_row)
    def _():
        pl.semaphore_signal(
            ready, inc=1, device_id=at(0, 1 - DEPTH), device_id_type=MESH
        )

    @each_group
    def _(g):
        along_inner(0, 2, g).start()
        along_inner(0, 1, g).start()

    for load in loads[2 * GROUPS :]:
        load.wait()
    for half in range(2):
        rows = slice(half * HALF, (half + 1) * HALF)
        for g in range(GROUPS):
            for j in range(SHARED):
                columns = slice((g * SHARED + j) * WIDTH, (g * SHARED + j + 1) * WIDTH)
                q[half, g, j * HALF : (j + 1) * HALF] = q_all[rows, columns]
                do[half, g, j * HALF : (j + 1) * HALF] = do_all[rows, columns]
    low_lane = lax.broadcasted_iota(jnp.int32, (1, WIDTH), 1) < HALF
    for source, target, factor in ((norm_ref, norm, LOG2E), (dot_ref, dot, 1.0)):
        straight = source[0] * factor
        swapped = pltpu.roll(straight, HALF, 1)
        for g in range(GROUPS):
            for j in range(0, SHARED, 2):
                a, b = g * SHARED + j, g * SHARED + j + 1
                columns = slice(j * HALF, (j + 2) * HALF)
                target[0, g, :, columns] = jnp.where(
                    low_lane, straight[a : a + 1], swapped[b : b + 1]
                )
                target[1, g, :, columns] = jnp.where(
                    low_lane, swapped[a : a + 1], straight[b : b + 1]
                )

    def block_of(slot):
        there = at(-(slot % 3), -(slot // 3))
        return there["inner"] * n_outer + there["outer"]

    def cover(slot, half):
        seen = off_ref[half, block_of(slot)] < off_ref[half, block_of(0)]
        return jnp.where(seen, 0.0, HIDDEN).astype(F32)

    within = lax.broadcasted_iota(jnp.int32, (HALF, ROWS), 0) <= (
        lax.broadcasted_iota(jnp.int32, (HALF, ROWS), 1) % HALF
    )

    def tile(half, g, keys, values, slots, kinds):
        queries, grads = q[half, g], do[half, g]
        bias = norm[half, g]
        scores = product(keys, queries, 1, 1) * (SCALE * LOG2E)
        pieces = []
        for n, (slot, key_half) in enumerate(kinds):
            piece = scores[n * HALF : (n + 1) * HALF]
            if key_half != half:
                piece = jnp.exp2(piece - bias)
            elif slot == 0:
                piece = jnp.where(within, jnp.exp2(piece - bias), 0.0)
            else:
                piece = jnp.exp2(piece - (bias + cover(slot, half)))
            pieces.append(piece)
        probs = jnp.concatenate(pieces, 0)
        grad_probs = product(values, grads, 1, 1)
        grad_scores = (probs * (grad_probs - dot[half, g])).astype(BF16)
        probs = probs.astype(BF16)
        grad_value = product(probs, grads, 1, 0)
        grad_key = product(grad_scores, queries, 1, 0)
        term = product(grad_scores, keys, 0, 0)
        dq[half, g] = term if slots[0] == 0 else dq[half, g] + term
        return grad_key, grad_value

    def compute(slots, g):
        here = pl.ds(slots[0] * WIDTH, len(slots) * WIDTH)
        keys, values = kv[g, 0, here], kv[g, 1, here]
        count = range(len(slots))
        early = lambda x: jnp.concatenate([x[n * WIDTH : n * WIDTH + HALF] for n in count], 0)
        late_side = tile(1, g, keys, values, slots, [(s, kh) for s in slots for kh in (0, 1)])
        early_side = tile(0, g, early(keys), early(values), slots, [(s, 0) for s in slots])
        sums = []
        for n in count:
            both = []
            for a, b in zip(late_side, early_side):
                low = a[n * WIDTH : n * WIDTH + HALF] + b[n * HALF : (n + 1) * HALF]
                both.append((low, a[n * WIDTH + HALF : (n + 1) * WIDTH]))
            sums.append(both)
        return sums

    def put(ref, lead, pair):
        for kind, factor in ((0, SCALE), (1, 1.0)):
            for half in range(2):
                rows = slice(half * HALF, (half + 1) * HALF)
                ref[(*lead, kind, rows)] = (pair[kind][half] * factor).astype(ref.dtype)

    def pair_of_slots(row, g):
        one, two = compute((3 * row + 1, 3 * row + 2), g)
        put(back, (2 * row + 1, g), two)
        returned(3 * row + 2, g).start()
        put(back, (2 * row, g), one)
        returned(3 * row + 1, g).start()

    along_outer(0).wait_send()
    along_outer(1).start()

    @each_group
    def _(g):
        put(part, (0, g), compute((0,), g)[0])

    @each_group
    def _(g):
        along_inner(0, 1, g).wait_recv()
        along_inner(0, 2, g).wait_recv()
        pair_of_slots(0, g)

    @each_group
    def _(g):
        along_outer(g).wait_recv()
        along_inner(1, 2, g).start()
        along_inner(1, 1, g).start()
        put(part, (1, g), compute((3,), g)[0])

    def collect(row, g):
        returned(3 * row + 1, g).wait_recv()
        returned(3 * row + 2, g).wait_recv()
        return part[row, g] + got[2 * row, g].astype(F32) + got[2 * row + 1, g].astype(F32)

    @each_group
    def _(g):
        part[0, g] = collect(0, g)
        hst[g] = part[0, g, :, pl.ds(other * HALF, HALF)].astype(BF16)
        head_copy(g).start()

    @each_group
    def _(g):
        along_inner(1, 1, g).wait_recv()
        along_inner(1, 2, g).wait_recv()
        pair_of_slots(1, g)
        first = h * (GROUPS * SHARED * WIDTH) + g * (SHARED * WIDTH)
        for j in range(SHARED):
            rows = slice(j * HALF, (j + 1) * HALF)
            qst[g, :, j * WIDTH : (j + 1) * WIDTH] = (dq[other, g, rows] * SCALE).astype(BF16)
        query_copy(g).start()
        for j in range(SHARED):
            rows = slice(j * HALF, (j + 1) * HALF)
            columns = pl.ds(pl.multiple_of(first + j * WIDTH, WIDTH), WIDTH)
            oq_ref[0, :, columns] = (dq[h, g, rows] * SCALE).astype(BF16)

    @pl.when(first_of_row)
    def _():
        pl.semaphore_wait(ready, 1)

    @each_group
    def _(g):
        zst[g] = collect(1, g).astype(BF16)

        @pl.when(first_of_row)
        def _():
            relay_copy(g).start()

        @pl.when(not_first)
        def _():
            outer_return(0, g).start()
            outer_return(1, g).start()

    @each_group
    def _(g):
        query_copy(g).wait_recv()
        first = other * (GROUPS * SHARED * WIDTH) + g * (SHARED * WIDTH)
        columns = pl.ds(pl.multiple_of(first, WIDTH), SHARED * WIDTH)
        oq_ref[0, :, columns] = qgot[g]

    @pl.when(last_of_row)
    def _():
        @each_group
        def _(g):
            relay_copy(g).wait_recv()
            relay_onward(0, g).start()
            relay_onward(1, g).start()

    @each_group
    def _(g):
        mine = pl.ds(pl.multiple_of(h * (GROUPS * WIDTH) + g * WIDTH, WIDTH), WIDTH)
        theirs = pl.ds(pl.multiple_of(other * (GROUPS * WIDTH) + g * WIDTH, WIDTH), WIDTH)
        head_copy(g).wait_recv()
        outer_arrival(0, g).wait_recv()
        outer_arrival(1, g).wait_recv()
        for kind, ref in ((0, ok_ref), (1, ov_ref)):
            own = part[0, g, kind, pl.ds(h * HALF, HALF)] + zgot[h, g, kind].astype(F32)
            ref[0, :, mine] = own.astype(BF16)
            far = hgot[g, kind].astype(F32) + zgot[other, g, kind].astype(F32)
            ref[0, :, theirs] = far.astype(BF16)

    along_outer(1).wait_send()

    @each_group
    def _(g):
        for row in range(2):
            for step in (1, 2):
                along_inner(row, step, g).wait_send()
                returned(3 * row + step, g).wait_send()
        head_copy(g).wait_send()
        query_copy(g).wait_send()

        @pl.when(first_of_row)
        def _():
            relay_copy(g).wait_send()

        @pl.when(not_first)
        def _():
            outer_return(0, g).wait_send()
            outer_return(1, g).wait_send()

        @pl.when(last_of_row)
        def _():
            relay_onward(0, g).wait_send()
            relay_onward(1, g).wait_send()


def place_kernel(*refs):
    count = (len(refs) - 1) // 2
    copies = [
        pltpu.make_async_copy(refs[n], refs[count + n], refs[-1].at[n]) for n in range(count)
    ]
    for copy in copies:
        copy.start()
    for copy in copies:
        copy.wait()


def solution(mesh):
    n_inner, n_outer = mesh.shape["inner"], mesh.shape["outer"]
    vmem = pl.BlockSpec(memory_space=pltpu.VMEM)
    hbm = pl.BlockSpec(memory_space=pltpu.HBM)
    square = (2, WIDTH, WIDTH)
    part_half = (2, HALF, WIDTH)
    dma = pltpu.SemaphoreType.DMA

    def shards(queries, keys, values, grad_out, log_denominator, row_dot, offsets):
        columns = GROUPS * SHARED * WIDTH
        shapes = [
            jax.ShapeDtypeStruct((1, HALF, 2 * columns), BF16),
            jax.ShapeDtypeStruct((1, HALF, 2 * GROUPS * WIDTH), BF16),
            jax.ShapeDtypeStruct((1, HALF, 2 * GROUPS * WIDTH), BF16),
        ]
        sums = pl.pallas_call(
            functools.partial(kernel, n_inner, n_outer),
            out_shape=[pltpu.VMEM(shape.shape, shape.dtype) for shape in shapes],
            in_specs=[hbm] * 4 + [vmem] * 2 + [pl.BlockSpec(memory_space=pltpu.SMEM)],
            out_specs=[vmem] * 3,
            scratch_shapes=[
                pltpu.VMEM((WIDTH, columns), BF16),
                pltpu.VMEM((WIDTH, columns), BF16),
                pltpu.VMEM((2, GROUPS, ROWS, WIDTH), BF16),
                pltpu.VMEM((2, GROUPS, ROWS, WIDTH), BF16),
                pltpu.VMEM((2, GROUPS, 1, ROWS), F32),
                pltpu.VMEM((2, GROUPS, 1, ROWS), F32),
                pltpu.VMEM((2, GROUPS, ROWS, WIDTH), F32),
                pltpu.VMEM((GROUPS, 2, 6 * WIDTH, WIDTH), BF16),
                pltpu.VMEM((2, GROUPS, *square), F32),
                pltpu.VMEM((4, GROUPS, *square), BF16),
                pltpu.VMEM((4, GROUPS, *square), BF16),
                pltpu.VMEM((GROUPS, *square), BF16),
                pltpu.VMEM((GROUPS, *square), BF16),
                pltpu.VMEM((2, GROUPS, *part_half), BF16),
                pltpu.VMEM((GROUPS, *part_half), BF16),
                pltpu.VMEM((GROUPS, *part_half), BF16),
                pltpu.VMEM((GROUPS, HALF, SHARED * WIDTH), BF16),
                pltpu.VMEM((GROUPS, HALF, SHARED * WIDTH), BF16),
                dma((5, GROUPS)),
                dma((5, GROUPS)),
                dma((4, GROUPS)),
                dma((4, GROUPS)),
                dma((2, GROUPS)),
                dma((2, GROUPS)),
                dma((GROUPS,)),
                dma((GROUPS,)),
                dma((GROUPS,)),
                dma((GROUPS,)),
                dma((GROUPS,)),
                dma((GROUPS,)),
                dma((2, GROUPS)),
                pltpu.SemaphoreType.REGULAR,
                dma((2 * GROUPS + 2,)),
            ],
            compiler_params=pltpu.CompilerParams(
                collective_id=0, has_side_effects=True, vmem_limit_bytes=56 << 20
            ),
        )(
            queries,
            keys,
            values,
            grad_out,
            jnp.swapaxes(log_denominator, 1, 2),
            jnp.swapaxes(row_dot, 1, 2),
            offsets.T,
        )
        return pl.pallas_call(
            place_kernel,
            out_shape=shapes,
            in_specs=[vmem] * 3,
            out_specs=[pl.BlockSpec(memory_space=pl.ANY)] * 3,
            scratch_shapes=[dma((3,))],
            compiler_params=pltpu.CompilerParams(vmem_limit_bytes=4 << 20),
        )(*sums)

    spec_in = P(("inner", "outer"), None, "head")
    spec_out = P(("inner", "outer"), "head", None)
    return jax.shard_map(
        shards,
        mesh=mesh,
        in_specs=(spec_in,) * 6 + (P(),),
        out_specs=(spec_out,) * 3,
        check_vma=False,
    )
```

```python
import functools
import math

import jax
import jax.numpy as jnp
from jax import lax
from jax.experimental import pallas as pl
from jax.experimental.pallas import tpu as pltpu
from jax.sharding import PartitionSpec as P

MESH = pl.DeviceIdType.MESH
F32 = jnp.float32
BF16 = jnp.bfloat16
WIDTH = 128
HALF = 64
GROUPS = 2
SHARED = 8
ROWS = SHARED * HALF
SCALE = 1.0 / math.sqrt(WIDTH)
LOG2E = math.log2(math.e)
DEPTH = 8
HIDDEN = 1.0e5


def product(a, b, dim_a, dim_b):
    return lax.dot_general(
        a, b, (((dim_a,), (dim_b,)), ((), ())), preferred_element_type=F32
    )


def kernel(
    n_inner,
    n_outer,
    q_ref,
    k_ref,
    v_ref,
    do_ref,
    norm_ref,
    dot_ref,
    off_ref,
    oq_ref,
    ok_ref,
    ov_ref,
    q_all,
    do_all,
    q,
    do,
    norm,
    dot,
    dq,
    kv,
    part,
    back,
    got,
    zst,
    relay,
    zrel,
    zgot,
    hst,
    hgot,
    qst,
    qgot,
    kv_ss,
    kv_rs,
    bk_ss,
    bk_rs,
    z_ss,
    z_rs,
    h_ss,
    h_rs,
    q_ss,
    q_rs,
    r_ss,
    r_rs,
    f_ss,
    ready,
    in_sem,
):
    i, o, h = lax.axis_index("inner"), lax.axis_index("outer"), lax.axis_index("head")
    other = 1 - h

    def at(di=0, do_=0, head=None):
        return {
            "inner": lax.rem(i + (di + n_inner), n_inner),
            "outer": lax.rem(o + (do_ + n_outer), n_outer),
            "head": h if head is None else head,
        }

    loads = []
    for kind, ref in ((0, k_ref), (1, v_ref)):
        for g in range(GROUPS):
            loads.append((ref.at[0, :, pl.ds(g * WIDTH, WIDTH)], kv.at[g, kind, pl.ds(0, WIDTH)]))
    loads += [(q_ref.at[0], q_all), (do_ref.at[0], do_all)]
    loads = [
        pltpu.make_async_copy(source, target, in_sem.at[n])
        for n, (source, target) in enumerate(loads)
    ]
    for load in loads:
        load.start()

    barrier = pltpu.get_barrier_semaphore()
    place = lax.rem(o, DEPTH)
    first_of_row, last_of_row = place == 0, place == DEPTH - 1
    not_first, not_last = jnp.logical_not(first_of_row), jnp.logical_not(last_of_row)

    def greet(devices):
        for device in devices:
            pl.semaphore_signal(barrier, inc=1, device_id=device, device_id_type=MESH)

    greet([at(0, -1), at(0, 0, other), at(1), at(-1), at(2), at(-2)])

    @pl.when(not_last)
    def _():
        greet([at(0, 1), at(0, 1, other)])

    @pl.when(first_of_row)
    def _():
        greet([at(-step, DEPTH - 1) for step in range(3)])

    @pl.when(last_of_row)
    def _():
        greet([at(0, DEPTH, 0), at(0, DEPTH, 1)])

    for load in loads[: 2 * GROUPS]:
        load.wait()

    greeted = 6 + jnp.where(not_first, 2, 0) + jnp.where(last_of_row, 5, 0)
    pl.semaphore_wait(barrier, greeted)

    def slot_copy(source, target, g, device):
        return pltpu.make_async_remote_copy(
            src_ref=kv.at[g, :, pl.ds(source * WIDTH, WIDTH)],
            dst_ref=kv.at[g, :, pl.ds(target * WIDTH, WIDTH)],
            send_sem=kv_ss.at[target - 1, g],
            recv_sem=kv_rs.at[target - 1, g],
            device_id=device,
            device_id_type=MESH,
        )

    def along_outer(g):
        return slot_copy(0, 3, g, at(0, 1))

    def along_inner(row, step, g):
        return slot_copy(3 * row, 3 * row + step, g, at(step))

    def returned(slot, g):
        step = slot % 3
        return pltpu.make_async_remote_copy(
            src_ref=back.at[slot // 3 * 2 + step - 1, g],
            dst_ref=got.at[slot // 3 * 2 + step - 1, g],
            send_sem=bk_ss.at[slot // 3 * 2 + step - 1, g],
            recv_sem=bk_rs.at[slot // 3 * 2 + step - 1, g],
            device_id=at(-step),
            device_id_type=MESH,
        )

    def outer_return(half, g):
        return pltpu.make_async_remote_copy(
            src_ref=zst.at[g, :, pl.ds(half * HALF, HALF)],
            dst_ref=zgot.at[h, g],
            send_sem=z_ss.at[half, g],
            recv_sem=z_rs.at[h, g],
            device_id=at(0, -1, half),
            device_id_type=MESH,
        )

    def outer_arrival(head, g):
        return pltpu.make_async_remote_copy(
            src_ref=zst.at[g, :, pl.ds(0, HALF)],
            dst_ref=zgot.at[head, g],
            send_sem=z_ss.at[0, g],
            recv_sem=z_rs.at[head, g],
            device_id=at(0, -1),
            device_id_type=MESH,
        )

    def relay_copy(step, g):
        return pltpu.make_async_remote_copy(
            src_ref=back.at[1 + step, g] if step else zst.at[g],
            dst_ref=relay.at[step, g],
            send_sem=r_ss.at[step, g],
            recv_sem=r_rs.at[step, g],
            device_id=at(-step, DEPTH - 1),
            device_id_type=MESH,
        )

    def relay_onward(half, g):
        return pltpu.make_async_remote_copy(
            src_ref=zrel.at[g, :, pl.ds(half * HALF, HALF)],
            dst_ref=zgot.at[h, g],
            send_sem=f_ss.at[half, g],
            recv_sem=z_rs.at[h, g],
            device_id=at(0, -DEPTH, half),
            device_id_type=MESH,
        )

    def head_copy(g):
        return pltpu.make_async_remote_copy(
            src_ref=hst.at[g],
            dst_ref=hgot.at[g],
            send_sem=h_ss.at[g],
            recv_sem=h_rs.at[g],
            device_id=at(0, 0, other),
            device_id_type=MESH,
        )

    def query_copy(g):
        return pltpu.make_async_remote_copy(
            src_ref=qst.at[g],
            dst_ref=qgot.at[g],
            send_sem=q_ss.at[g],
            recv_sem=q_rs.at[g],
            device_id=at(0, 0, other),
            device_id_type=MESH,
        )

    def each_group(body):
        def step(g, carry):
            body(g)
            return carry

        lax.fori_loop(0, GROUPS, step, 0)

    along_outer(0).start()

    @pl.when(last_of_row)
    def _():
        for step in range(3):
            first = at(step, 1 - DEPTH)
            pl.semaphore_signal(ready, inc=1, device_id=first, device_id_type=MESH)

    @each_group
    def _(g):
        along_inner(0, 2, g).start()
        along_inner(0, 1, g).start()

    for load in loads[2 * GROUPS :]:
        load.wait()
    for half in range(2):
        rows = slice(half * HALF, (half + 1) * HALF)
        for g in range(GROUPS):
            for j in range(SHARED):
                columns = slice((g * SHARED + j) * WIDTH, (g * SHARED + j + 1) * WIDTH)
                q[half, g, j * HALF : (j + 1) * HALF] = q_all[rows, columns]
                do[half, g, j * HALF : (j + 1) * HALF] = do_all[rows, columns]
    low_lane = lax.broadcasted_iota(jnp.int32, (1, WIDTH), 1) < HALF
    for source, target, factor in ((norm_ref, norm, LOG2E), (dot_ref, dot, 1.0)):
        straight = source[0] * factor
        swapped = pltpu.roll(straight, HALF, 1)
        for g in range(GROUPS):
            for j in range(0, SHARED, 2):
                a, b = g * SHARED + j, g * SHARED + j + 1
                columns = slice(j * HALF, (j + 2) * HALF)
                target[0, g, :, columns] = jnp.where(
                    low_lane, straight[a : a + 1], swapped[b : b + 1]
                )
                target[1, g, :, columns] = jnp.where(
                    low_lane, swapped[a : a + 1], straight[b : b + 1]
                )

    def block_of(slot):
        there = at(-(slot % 3), -(slot // 3))
        return there["inner"] * n_outer + there["outer"]

    def cover(slot, half):
        seen = off_ref[half, block_of(slot)] < off_ref[half, block_of(0)]
        return jnp.where(seen, 0.0, HIDDEN).astype(F32)

    within = lax.broadcasted_iota(jnp.int32, (HALF, ROWS), 0) <= (
        lax.broadcasted_iota(jnp.int32, (HALF, ROWS), 1) % HALF
    )

    def tile(half, g, keys, values, slots, kinds):
        queries, grads = q[half, g], do[half, g]
        bias = norm[half, g]
        scores = product(keys, queries, 1, 1) * (SCALE * LOG2E)
        pieces = []
        for n, (slot, key_half) in enumerate(kinds):
            piece = scores[n * HALF : (n + 1) * HALF]
            if key_half != half:
                piece = jnp.exp2(piece - bias)
            elif slot == 0:
                piece = jnp.where(within, jnp.exp2(piece - bias), 0.0)
            else:
                piece = jnp.exp2(piece - (bias + cover(slot, half)))
            pieces.append(piece)
        probs = jnp.concatenate(pieces, 0)
        grad_probs = product(values, grads, 1, 1)
        grad_scores = (probs * (grad_probs - dot[half, g])).astype(BF16)
        probs = probs.astype(BF16)
        grad_value = product(probs, grads, 1, 0)
        grad_key = product(grad_scores, queries, 1, 0)
        term = product(grad_scores, keys, 0, 0)
        dq[half, g] = term if slots[0] == 0 else dq[half, g] + term
        return grad_key, grad_value

    def compute(slots, g):
        here = pl.ds(slots[0] * WIDTH, len(slots) * WIDTH)
        keys, values = kv[g, 0, here], kv[g, 1, here]
        count = range(len(slots))
        early = lambda x: jnp.concatenate([x[n * WIDTH : n * WIDTH + HALF] for n in count], 0)
        late_side = tile(1, g, keys, values, slots, [(s, kh) for s in slots for kh in (0, 1)])
        early_side = tile(0, g, early(keys), early(values), slots, [(s, 0) for s in slots])
        sums = []
        for n in count:
            both = []
            for a, b in zip(late_side, early_side):
                low = a[n * WIDTH : n * WIDTH + HALF] + b[n * HALF : (n + 1) * HALF]
                both.append((low, a[n * WIDTH + HALF : (n + 1) * WIDTH]))
            sums.append(both)
        return sums

    def put(ref, lead, pair):
        for kind, factor in ((0, SCALE), (1, 1.0)):
            for half in range(2):
                rows = slice(half * HALF, (half + 1) * HALF)
                ref[(*lead, kind, rows)] = (pair[kind][half] * factor).astype(ref.dtype)

    def pair_of_slots(row, g):
        one, two = compute((3 * row + 1, 3 * row + 2), g)
        put(back, (2 * row + 1, g), two)
        put(back, (2 * row, g), one)
        if row == 0:
            returned(2, g).start()
            returned(1, g).start()
            return

        @pl.when(not_first)
        def _():
            returned(5, g).start()
            returned(4, g).start()

        @pl.when(first_of_row)
        def _():
            relay_copy(2, g).start()
            relay_copy(1, g).start()

    along_outer(0).wait_send()
    along_outer(1).start()

    @each_group
    def _(g):
        put(part, (0, g), compute((0,), g)[0])

    @each_group
    def _(g):
        along_inner(0, 1, g).wait_recv()
        along_inner(0, 2, g).wait_recv()
        pair_of_slots(0, g)

    @pl.when(first_of_row)
    def _():
        pl.semaphore_wait(ready, 3)

    @each_group
    def _(g):
        along_outer(g).wait_recv()
        along_inner(1, 2, g).start()
        along_inner(1, 1, g).start()
        put(part, (1, g), compute((3,), g)[0])

        @pl.when(first_of_row)
        def _():
            zst[g] = part[1, g].astype(BF16)
            relay_copy(0, g).start()

    def collect(row, g):
        returned(3 * row + 1, g).wait_recv()
        returned(3 * row + 2, g).wait_recv()
        return part[row, g] + got[2 * row, g].astype(F32) + got[2 * row + 1, g].astype(F32)

    @each_group
    def _(g):
        part[0, g] = collect(0, g)
        hst[g] = part[0, g, :, pl.ds(other * HALF, HALF)].astype(BF16)
        head_copy(g).start()

    @each_group
    def _(g):
        along_inner(1, 1, g).wait_recv()
        along_inner(1, 2, g).wait_recv()
        pair_of_slots(1, g)
        first = h * (GROUPS * SHARED * WIDTH) + g * (SHARED * WIDTH)
        for j in range(SHARED):
            rows = slice(j * HALF, (j + 1) * HALF)
            qst[g, :, j * WIDTH : (j + 1) * WIDTH] = (dq[other, g, rows] * SCALE).astype(BF16)
        query_copy(g).start()
        for j in range(SHARED):
            rows = slice(j * HALF, (j + 1) * HALF)
            columns = pl.ds(pl.multiple_of(first + j * WIDTH, WIDTH), WIDTH)
            oq_ref[0, :, columns] = (dq[h, g, rows] * SCALE).astype(BF16)

    @pl.when(not_first)
    def _():
        @each_group
        def _(g):
            zst[g] = collect(1, g).astype(BF16)
            outer_return(0, g).start()
            outer_return(1, g).start()

    @each_group
    def _(g):
        query_copy(g).wait_recv()
        first = other * (GROUPS * SHARED * WIDTH) + g * (SHARED * WIDTH)
        columns = pl.ds(pl.multiple_of(first, WIDTH), SHARED * WIDTH)
        oq_ref[0, :, columns] = qgot[g]

    @pl.when(last_of_row)
    def _():
        @each_group
        def _(g):
            for step in range(3):
                relay_copy(step, g).wait_recv()
            zrel[g] = sum(relay[step, g].astype(F32) for step in range(3)).astype(BF16)
            relay_onward(0, g).start()
            relay_onward(1, g).start()

    @each_group
    def _(g):
        mine = pl.ds(pl.multiple_of(h * (GROUPS * WIDTH) + g * WIDTH, WIDTH), WIDTH)
        theirs = pl.ds(pl.multiple_of(other * (GROUPS * WIDTH) + g * WIDTH, WIDTH), WIDTH)
        head_copy(g).wait_recv()
        outer_arrival(0, g).wait_recv()
        outer_arrival(1, g).wait_recv()
        for kind, ref in ((0, ok_ref), (1, ov_ref)):
            own = part[0, g, kind, pl.ds(h * HALF, HALF)] + zgot[h, g, kind].astype(F32)
            ref[0, :, mine] = own.astype(BF16)
            far = hgot[g, kind].astype(F32) + zgot[other, g, kind].astype(F32)
            ref[0, :, theirs] = far.astype(BF16)

    along_outer(1).wait_send()

    @each_group
    def _(g):
        for step in (1, 2):
            along_inner(0, step, g).wait_send()
            along_inner(1, step, g).wait_send()
            returned(step, g).wait_send()
        head_copy(g).wait_send()
        query_copy(g).wait_send()

        @pl.when(first_of_row)
        def _():
            for step in range(3):
                relay_copy(step, g).wait_send()

        @pl.when(not_first)
        def _():
            returned(4, g).wait_send()
            returned(5, g).wait_send()
            outer_return(0, g).wait_send()
            outer_return(1, g).wait_send()

        @pl.when(last_of_row)
        def _():
            relay_onward(0, g).wait_send()
            relay_onward(1, g).wait_send()


def place_kernel(*refs):
    count = (len(refs) - 1) // 2
    copies = [
        pltpu.make_async_copy(refs[n], refs[count + n], refs[-1].at[n]) for n in range(count)
    ]
    for copy in copies:
        copy.start()
    for copy in copies:
        copy.wait()


def solution(mesh):
    n_inner, n_outer = mesh.shape["inner"], mesh.shape["outer"]
    vmem = pl.BlockSpec(memory_space=pltpu.VMEM)
    hbm = pl.BlockSpec(memory_space=pltpu.HBM)
    square = (2, WIDTH, WIDTH)
    part_half = (2, HALF, WIDTH)
    dma = pltpu.SemaphoreType.DMA

    def shards(queries, keys, values, grad_out, log_denominator, row_dot, offsets):
        columns = GROUPS * SHARED * WIDTH
        shapes = [
            jax.ShapeDtypeStruct((1, HALF, 2 * columns), BF16),
            jax.ShapeDtypeStruct((1, HALF, 2 * GROUPS * WIDTH), BF16),
            jax.ShapeDtypeStruct((1, HALF, 2 * GROUPS * WIDTH), BF16),
        ]
        sums = pl.pallas_call(
            functools.partial(kernel, n_inner, n_outer),
            out_shape=[pltpu.VMEM(shape.shape, shape.dtype) for shape in shapes],
            in_specs=[hbm] * 4 + [vmem] * 2 + [pl.BlockSpec(memory_space=pltpu.SMEM)],
            out_specs=[vmem] * 3,
            scratch_shapes=[
                pltpu.VMEM((WIDTH, columns), BF16),
                pltpu.VMEM((WIDTH, columns), BF16),
                pltpu.VMEM((2, GROUPS, ROWS, WIDTH), BF16),
                pltpu.VMEM((2, GROUPS, ROWS, WIDTH), BF16),
                pltpu.VMEM((2, GROUPS, 1, ROWS), F32),
                pltpu.VMEM((2, GROUPS, 1, ROWS), F32),
                pltpu.VMEM((2, GROUPS, ROWS, WIDTH), F32),
                pltpu.VMEM((GROUPS, 2, 6 * WIDTH, WIDTH), BF16),
                pltpu.VMEM((2, GROUPS, *square), F32),
                pltpu.VMEM((4, GROUPS, *square), BF16),
                pltpu.VMEM((4, GROUPS, *square), BF16),
                pltpu.VMEM((GROUPS, *square), BF16),
                pltpu.VMEM((3, GROUPS, *square), BF16),
                pltpu.VMEM((GROUPS, *square), BF16),
                pltpu.VMEM((2, GROUPS, *part_half), BF16),
                pltpu.VMEM((GROUPS, *part_half), BF16),
                pltpu.VMEM((GROUPS, *part_half), BF16),
                pltpu.VMEM((GROUPS, HALF, SHARED * WIDTH), BF16),
                pltpu.VMEM((GROUPS, HALF, SHARED * WIDTH), BF16),
                dma((5, GROUPS)),
                dma((5, GROUPS)),
                dma((4, GROUPS)),
                dma((4, GROUPS)),
                dma((2, GROUPS)),
                dma((2, GROUPS)),
                dma((GROUPS,)),
                dma((GROUPS,)),
                dma((GROUPS,)),
                dma((GROUPS,)),
                dma((3, GROUPS)),
                dma((3, GROUPS)),
                dma((2, GROUPS)),
                pltpu.SemaphoreType.REGULAR,
                dma((2 * GROUPS + 2,)),
            ],
            compiler_params=pltpu.CompilerParams(
                collective_id=0, has_side_effects=True, vmem_limit_bytes=56 << 20
            ),
        )(
            queries,
            keys,
            values,
            grad_out,
            jnp.swapaxes(log_denominator, 1, 2),
            jnp.swapaxes(row_dot, 1, 2),
            offsets.T,
        )
        return pl.pallas_call(
            place_kernel,
            out_shape=shapes,
            in_specs=[vmem] * 3,
            out_specs=[pl.BlockSpec(memory_space=pl.ANY)] * 3,
            scratch_shapes=[dma((3,))],
            compiler_params=pltpu.CompilerParams(vmem_limit_bytes=4 << 20),
        )(*sums)

    spec_in = P(("inner", "outer"), None, "head")
    spec_out = P(("inner", "outer"), "head", None)
    return jax.shard_map(
        shards,
        mesh=mesh,
        in_specs=(spec_in,) * 6 + (P(),),
        out_specs=(spec_out,) * 3,
        check_vma=False,
    )
```

```python
import functools
import math

import jax
import jax.numpy as jnp
from jax import lax
from jax.experimental import pallas as pl
from jax.experimental.pallas import tpu as pltpu
from jax.sharding import PartitionSpec as P

MESH = pl.DeviceIdType.MESH
F32 = jnp.float32
BF16 = jnp.bfloat16
WIDTH = 128
HALF = 64
GROUPS = 2
SHARED = 8
ROWS = SHARED * HALF
SCALE = 1.0 / math.sqrt(WIDTH)
LOG2E = math.log2(math.e)
DEPTH = 8
HIDDEN = 1.0e5


def product(a, b, dim_a, dim_b):
    return lax.dot_general(
        a, b, (((dim_a,), (dim_b,)), ((), ())), preferred_element_type=F32
    )


def kernel(
    n_inner,
    n_outer,
    q_ref,
    k_ref,
    v_ref,
    do_ref,
    norm_ref,
    dot_ref,
    off_ref,
    oq_ref,
    ok_ref,
    ov_ref,
    q_all,
    do_all,
    q,
    do,
    norm,
    dot,
    dq,
    kv,
    part,
    back,
    got,
    zst,
    relay,
    zrel,
    zgot,
    hst,
    hgot,
    qst,
    qgot,
    kv_ss,
    kv_rs,
    bk_ss,
    bk_rs,
    z_ss,
    z_rs,
    h_ss,
    h_rs,
    q_ss,
    q_rs,
    r_ss,
    r_rs,
    f_ss,
    ready,
    in_sem,
):
    i, o, h = lax.axis_index("inner"), lax.axis_index("outer"), lax.axis_index("head")
    other = 1 - h

    def at(di=0, do_=0, head=None):
        return {
            "inner": lax.rem(i + (di + n_inner), n_inner),
            "outer": lax.rem(o + (do_ + n_outer), n_outer),
            "head": h if head is None else head,
        }

    loads = []
    for kind, ref in ((0, k_ref), (1, v_ref)):
        for g in range(GROUPS):
            loads.append((ref.at[0, :, pl.ds(g * WIDTH, WIDTH)], kv.at[g, kind, pl.ds(0, WIDTH)]))
    loads += [(q_ref.at[0], q_all), (do_ref.at[0], do_all)]
    loads = [
        pltpu.make_async_copy(source, target, in_sem.at[n])
        for n, (source, target) in enumerate(loads)
    ]
    for load in loads:
        load.start()

    barrier = pltpu.get_barrier_semaphore()
    place = lax.rem(o, DEPTH)
    first_of_row, last_of_row = place == 0, place == DEPTH - 1
    not_first, not_last = jnp.logical_not(first_of_row), jnp.logical_not(last_of_row)

    def greet(devices):
        for device in devices:
            pl.semaphore_signal(barrier, inc=1, device_id=device, device_id_type=MESH)

    greet([at(0, -1), at(0, 0, other), at(-1), at(-2)])

    @pl.when(not_last)
    def _():
        greet([at(0, 1), at(0, 1, other)])

    @pl.when(first_of_row)
    def _():
        greet([at(-step, DEPTH - 1) for step in range(3)])

    @pl.when(last_of_row)
    def _():
        greet([at(0, DEPTH, 0), at(0, DEPTH, 1)])

    for load in loads[: 2 * GROUPS]:
        load.wait()

    greeted = 4 + jnp.where(not_first, 2, 0) + jnp.where(last_of_row, 5, 0)
    pl.semaphore_wait(barrier, greeted)

    def slot_copy(source, target, g, device):
        return pltpu.make_async_remote_copy(
            src_ref=kv.at[g, :, pl.ds(source * WIDTH, WIDTH)],
            dst_ref=kv.at[g, :, pl.ds(target * WIDTH, WIDTH)],
            send_sem=kv_ss.at[target - 1, g],
            recv_sem=kv_rs.at[target - 1, g],
            device_id=device,
            device_id_type=MESH,
        )

    def along_outer(g):
        return slot_copy(0, 3, g, at(0, 1))

    def along_inner(row, step, g):
        return slot_copy(3 * row, 3 * row + step, g, at(step))

    def returned(slot, g):
        step = slot % 3
        return pltpu.make_async_remote_copy(
            src_ref=back.at[slot // 3 * 2 + step - 1, g],
            dst_ref=got.at[slot // 3 * 2 + step - 1, g],
            send_sem=bk_ss.at[slot // 3 * 2 + step - 1, g],
            recv_sem=bk_rs.at[slot // 3 * 2 + step - 1, g],
            device_id=at(-step),
            device_id_type=MESH,
        )

    def outer_return(half, g):
        return pltpu.make_async_remote_copy(
            src_ref=zst.at[g, :, pl.ds(half * HALF, HALF)],
            dst_ref=zgot.at[h, g],
            send_sem=z_ss.at[half, g],
            recv_sem=z_rs.at[h, g],
            device_id=at(0, -1, half),
            device_id_type=MESH,
        )

    def outer_arrival(head, g):
        return pltpu.make_async_remote_copy(
            src_ref=zst.at[g, :, pl.ds(0, HALF)],
            dst_ref=zgot.at[head, g],
            send_sem=z_ss.at[0, g],
            recv_sem=z_rs.at[head, g],
            device_id=at(0, -1),
            device_id_type=MESH,
        )

    def relay_copy(step, g):
        return pltpu.make_async_remote_copy(
            src_ref=back.at[1 + step, g] if step else zst.at[g],
            dst_ref=relay.at[step, g],
            send_sem=r_ss.at[step, g],
            recv_sem=r_rs.at[step, g],
            device_id=at(-step, DEPTH - 1),
            device_id_type=MESH,
        )

    def relay_onward(half, g):
        return pltpu.make_async_remote_copy(
            src_ref=zrel.at[g, :, pl.ds(half * HALF, HALF)],
            dst_ref=zgot.at[h, g],
            send_sem=f_ss.at[half, g],
            recv_sem=z_rs.at[h, g],
            device_id=at(0, -DEPTH, half),
            device_id_type=MESH,
        )

    def head_copy(g):
        return pltpu.make_async_remote_copy(
            src_ref=hst.at[g],
            dst_ref=hgot.at[g],
            send_sem=h_ss.at[g],
            recv_sem=h_rs.at[g],
            device_id=at(0, 0, other),
            device_id_type=MESH,
        )

    def query_copy(g):
        return pltpu.make_async_remote_copy(
            src_ref=qst.at[g],
            dst_ref=qgot.at[g],
            send_sem=q_ss.at[g],
            recv_sem=q_rs.at[g],
            device_id=at(0, 0, other),
            device_id_type=MESH,
        )

    def each_group(body):
        def step(g, carry):
            body(g)
            return carry

        lax.fori_loop(0, GROUPS, step, 0)

    along_outer(0).start()

    @pl.when(last_of_row)
    def _():
        for step in range(3):
            first = at(step, 1 - DEPTH)
            pl.semaphore_signal(ready, inc=1, device_id=first, device_id_type=MESH)

    @each_group
    def _(g):
        along_inner(0, 2, g).start()
        along_inner(0, 1, g).start()

    for load in loads[2 * GROUPS :]:
        load.wait()
    for half in range(2):
        rows = slice(half * HALF, (half + 1) * HALF)
        for g in range(GROUPS):
            for j in range(SHARED):
                columns = slice((g * SHARED + j) * WIDTH, (g * SHARED + j + 1) * WIDTH)
                q[half, g, j * HALF : (j + 1) * HALF] = q_all[rows, columns]
                do[half, g, j * HALF : (j + 1) * HALF] = do_all[rows, columns]
    low_lane = lax.broadcasted_iota(jnp.int32, (1, WIDTH), 1) < HALF
    for source, target, factor in ((norm_ref, norm, LOG2E), (dot_ref, dot, 1.0)):
        straight = source[0] * factor
        swapped = pltpu.roll(straight, HALF, 1)
        for g in range(GROUPS):
            for j in range(0, SHARED, 2):
                a, b = g * SHARED + j, g * SHARED + j + 1
                columns = slice(j * HALF, (j + 2) * HALF)
                target[0, g, :, columns] = jnp.where(
                    low_lane, straight[a : a + 1], swapped[b : b + 1]
                )
                target[1, g, :, columns] = jnp.where(
                    low_lane, swapped[a : a + 1], straight[b : b + 1]
                )

    def block_of(slot):
        there = at(-(slot % 3), -(slot // 3))
        return there["inner"] * n_outer + there["outer"]

    def cover(slot, half):
        seen = off_ref[half, block_of(slot)] < off_ref[half, block_of(0)]
        return jnp.where(seen, 0.0, HIDDEN).astype(F32)

    within = lax.broadcasted_iota(jnp.int32, (HALF, ROWS), 0) <= (
        lax.broadcasted_iota(jnp.int32, (HALF, ROWS), 1) % HALF
    )

    def tile(half, g, keys, values, slots, kinds):
        queries, grads = q[half, g], do[half, g]
        bias = norm[half, g]
        scores = product(keys, queries, 1, 1) * (SCALE * LOG2E)
        pieces = []
        for n, (slot, key_half) in enumerate(kinds):
            piece = scores[n * HALF : (n + 1) * HALF]
            if key_half != half:
                piece = jnp.exp2(piece - bias)
            elif slot == 0:
                piece = jnp.where(within, jnp.exp2(piece - bias), 0.0)
            else:
                piece = jnp.exp2(piece - (bias + cover(slot, half)))
            pieces.append(piece)
        probs = jnp.concatenate(pieces, 0)
        grad_probs = product(values, grads, 1, 1)
        grad_scores = (probs * (grad_probs - dot[half, g])).astype(BF16)
        probs = probs.astype(BF16)
        grad_value = product(probs, grads, 1, 0)
        grad_key = product(grad_scores, queries, 1, 0)
        term = product(grad_scores, keys, 0, 0)
        dq[half, g] = term if slots[0] == 0 else dq[half, g] + term
        return grad_key, grad_value

    def compute(slots, g):
        here = pl.ds(slots[0] * WIDTH, len(slots) * WIDTH)
        keys, values = kv[g, 0, here], kv[g, 1, here]
        count = range(len(slots))
        early = lambda x: jnp.concatenate([x[n * WIDTH : n * WIDTH + HALF] for n in count], 0)
        late_side = tile(1, g, keys, values, slots, [(s, kh) for s in slots for kh in (0, 1)])
        early_side = tile(0, g, early(keys), early(values), slots, [(s, 0) for s in slots])
        sums = []
        for n in count:
            both = []
            for a, b in zip(late_side, early_side):
                low = a[n * WIDTH : n * WIDTH + HALF] + b[n * HALF : (n + 1) * HALF]
                both.append((low, a[n * WIDTH + HALF : (n + 1) * WIDTH]))
            sums.append(both)
        return sums

    def put(ref, lead, pair):
        for kind, factor in ((0, SCALE), (1, 1.0)):
            for half in range(2):
                rows = slice(half * HALF, (half + 1) * HALF)
                ref[(*lead, kind, rows)] = (pair[kind][half] * factor).astype(ref.dtype)

    def send_queries(g):
        for j in range(SHARED):
            rows = slice(j * HALF, (j + 1) * HALF)
            qst[g, :, j * WIDTH : (j + 1) * WIDTH] = (dq[other, g, rows] * SCALE).astype(BF16)
        query_copy(g).start()

    def pair_of_slots(row, g, first=lambda g: None):
        one, two = compute((3 * row + 1, 3 * row + 2), g)
        first(g)
        put(back, (2 * row + 1, g), two)
        put(back, (2 * row, g), one)
        if row == 0:
            returned(2, g).start()
            returned(1, g).start()
            return

        @pl.when(not_first)
        def _():
            returned(5, g).start()
            returned(4, g).start()

        @pl.when(first_of_row)
        def _():
            relay_copy(2, g).start()
            relay_copy(1, g).start()

    along_outer(0).wait_send()
    along_outer(1).start()

    @each_group
    def _(g):
        put(part, (0, g), compute((0,), g)[0])

    @each_group
    def _(g):
        along_inner(0, 1, g).wait_recv()
        along_inner(0, 2, g).wait_recv()
        pair_of_slots(0, g)

    @pl.when(first_of_row)
    def _():
        pl.semaphore_wait(ready, 3)

    @each_group
    def _(g):
        along_outer(g).wait_recv()
        along_inner(1, 2, g).start()
        along_inner(1, 1, g).start()
        put(part, (1, g), compute((3,), g)[0])

        @pl.when(first_of_row)
        def _():
            zst[g] = part[1, g].astype(BF16)
            relay_copy(0, g).start()

    def collect(row, g):
        returned(3 * row + 1, g).wait_recv()
        returned(3 * row + 2, g).wait_recv()
        return part[row, g] + got[2 * row, g].astype(F32) + got[2 * row + 1, g].astype(F32)

    @each_group
    def _(g):
        part[0, g] = collect(0, g)
        hst[g] = part[0, g, :, pl.ds(other * HALF, HALF)].astype(BF16)
        head_copy(g).start()

    @each_group
    def _(g):
        along_inner(1, 1, g).wait_recv()
        along_inner(1, 2, g).wait_recv()
        pair_of_slots(1, g, send_queries)

    @pl.when(not_first)
    def _():
        @each_group
        def _(g):
            zst[g] = collect(1, g).astype(BF16)
            outer_return(0, g).start()
            outer_return(1, g).start()

    @each_group
    def _(g):
        first = h * (GROUPS * SHARED * WIDTH) + g * (SHARED * WIDTH)
        for j in range(SHARED):
            rows = slice(j * HALF, (j + 1) * HALF)
            columns = pl.ds(pl.multiple_of(first + j * WIDTH, WIDTH), WIDTH)
            oq_ref[0, :, columns] = (dq[h, g, rows] * SCALE).astype(BF16)

    @each_group
    def _(g):
        query_copy(g).wait_recv()
        first = other * (GROUPS * SHARED * WIDTH) + g * (SHARED * WIDTH)
        columns = pl.ds(pl.multiple_of(first, WIDTH), SHARED * WIDTH)
        oq_ref[0, :, columns] = qgot[g]

    @pl.when(last_of_row)
    def _():
        @each_group
        def _(g):
            for step in range(3):
                relay_copy(step, g).wait_recv()
            zrel[g] = sum(relay[step, g].astype(F32) for step in range(3)).astype(BF16)
            relay_onward(0, g).start()
            relay_onward(1, g).start()

    @each_group
    def _(g):
        mine = pl.ds(pl.multiple_of(h * (GROUPS * WIDTH) + g * WIDTH, WIDTH), WIDTH)
        theirs = pl.ds(pl.multiple_of(other * (GROUPS * WIDTH) + g * WIDTH, WIDTH), WIDTH)
        head_copy(g).wait_recv()
        outer_arrival(0, g).wait_recv()
        outer_arrival(1, g).wait_recv()
        for kind, ref in ((0, ok_ref), (1, ov_ref)):
            own = part[0, g, kind, pl.ds(h * HALF, HALF)] + zgot[h, g, kind].astype(F32)
            ref[0, :, mine] = own.astype(BF16)
            far = hgot[g, kind].astype(F32) + zgot[other, g, kind].astype(F32)
            ref[0, :, theirs] = far.astype(BF16)

    along_outer(1).wait_send()

    @each_group
    def _(g):
        for step in (1, 2):
            along_inner(0, step, g).wait_send()
            along_inner(1, step, g).wait_send()
            returned(step, g).wait_send()
        head_copy(g).wait_send()
        query_copy(g).wait_send()

        @pl.when(first_of_row)
        def _():
            for step in range(3):
                relay_copy(step, g).wait_send()

        @pl.when(not_first)
        def _():
            returned(4, g).wait_send()
            returned(5, g).wait_send()
            outer_return(0, g).wait_send()
            outer_return(1, g).wait_send()

        @pl.when(last_of_row)
        def _():
            relay_onward(0, g).wait_send()
            relay_onward(1, g).wait_send()


def place_kernel(*refs):
    count = (len(refs) - 1) // 2
    copies = [
        pltpu.make_async_copy(refs[n], refs[count + n], refs[-1].at[n]) for n in range(count)
    ]
    for copy in copies:
        copy.start()
    for copy in copies:
        copy.wait()


def solution(mesh):
    n_inner, n_outer = mesh.shape["inner"], mesh.shape["outer"]
    vmem = pl.BlockSpec(memory_space=pltpu.VMEM)
    hbm = pl.BlockSpec(memory_space=pltpu.HBM)
    square = (2, WIDTH, WIDTH)
    part_half = (2, HALF, WIDTH)
    dma = pltpu.SemaphoreType.DMA

    def shards(queries, keys, values, grad_out, log_denominator, row_dot, offsets):
        columns = GROUPS * SHARED * WIDTH
        shapes = [
            jax.ShapeDtypeStruct((1, HALF, 2 * columns), BF16),
            jax.ShapeDtypeStruct((1, HALF, 2 * GROUPS * WIDTH), BF16),
            jax.ShapeDtypeStruct((1, HALF, 2 * GROUPS * WIDTH), BF16),
        ]
        sums = pl.pallas_call(
            functools.partial(kernel, n_inner, n_outer),
            out_shape=[pltpu.VMEM(shape.shape, shape.dtype) for shape in shapes],
            in_specs=[hbm] * 4 + [vmem] * 2 + [pl.BlockSpec(memory_space=pltpu.SMEM)],
            out_specs=[vmem] * 3,
            scratch_shapes=[
                pltpu.VMEM((WIDTH, columns), BF16),
                pltpu.VMEM((WIDTH, columns), BF16),
                pltpu.VMEM((2, GROUPS, ROWS, WIDTH), BF16),
                pltpu.VMEM((2, GROUPS, ROWS, WIDTH), BF16),
                pltpu.VMEM((2, GROUPS, 1, ROWS), F32),
                pltpu.VMEM((2, GROUPS, 1, ROWS), F32),
                pltpu.VMEM((2, GROUPS, ROWS, WIDTH), F32),
                pltpu.VMEM((GROUPS, 2, 6 * WIDTH, WIDTH), BF16),
                pltpu.VMEM((2, GROUPS, *square), F32),
                pltpu.VMEM((4, GROUPS, *square), BF16),
                pltpu.VMEM((4, GROUPS, *square), BF16),
                pltpu.VMEM((GROUPS, *square), BF16),
                pltpu.VMEM((3, GROUPS, *square), BF16),
                pltpu.VMEM((GROUPS, *square), BF16),
                pltpu.VMEM((2, GROUPS, *part_half), BF16),
                pltpu.VMEM((GROUPS, *part_half), BF16),
                pltpu.VMEM((GROUPS, *part_half), BF16),
                pltpu.VMEM((GROUPS, HALF, SHARED * WIDTH), BF16),
                pltpu.VMEM((GROUPS, HALF, SHARED * WIDTH), BF16),
                dma((5, GROUPS)),
                dma((5, GROUPS)),
                dma((4, GROUPS)),
                dma((4, GROUPS)),
                dma((2, GROUPS)),
                dma((2, GROUPS)),
                dma((GROUPS,)),
                dma((GROUPS,)),
                dma((GROUPS,)),
                dma((GROUPS,)),
                dma((3, GROUPS)),
                dma((3, GROUPS)),
                dma((2, GROUPS)),
                pltpu.SemaphoreType.REGULAR,
                dma((2 * GROUPS + 2,)),
            ],
            compiler_params=pltpu.CompilerParams(
                collective_id=0, has_side_effects=True, vmem_limit_bytes=56 << 20
            ),
        )(
            queries,
            keys,
            values,
            grad_out,
            jnp.swapaxes(log_denominator, 1, 2),
            jnp.swapaxes(row_dot, 1, 2),
            offsets.T,
        )
        return pl.pallas_call(
            place_kernel,
            out_shape=shapes,
            in_specs=[vmem] * 3,
            out_specs=[pl.BlockSpec(memory_space=pl.ANY)] * 3,
            scratch_shapes=[dma((3,))],
            compiler_params=pltpu.CompilerParams(vmem_limit_bytes=4 << 20),
        )(*sums)

    spec_in = P(("inner", "outer"), None, "head")
    spec_out = P(("inner", "outer"), "head", None)
    return jax.shard_map(
        shards,
        mesh=mesh,
        in_specs=(spec_in,) * 6 + (P(),),
        out_specs=(spec_out,) * 3,
        check_vma=False,
    )
```
